128 devices in a mesh: wide: 32 (over x, y, core), narrow: 4 (over z).
Axes of the slice: x: 4, y: 4, z: 4, core: 2. Of those that a mesh axis runs over, the one named last changes fastest.
Arguments:
- cache: bfloat16 [32, 8192, 128], P('wide', 'narrow'), may hold values from -6 to 6
- lookup_slots: int32 [32, 16384, 16], P('wide'), may hold values from 0 to 8191
- bag_lengths: int32 [32, 16384], P('wide'), may hold values from 1 to 16
- miss_rows: bfloat16 [32, 4096, 128], P('wide', 'narrow'), may hold values from -6 to 6
- miss_slots: int32 [32, 4096], P('wide', 'narrow'), may hold values from 0 to 8191, as said below
- holder_counts: int32 [32, 16], P('wide', 'narrow'), may hold values from 0 to 512, as said below
- w_first: bfloat16 [4096, 4096], P(None, 'narrow'), may hold values from -0.09375 to 0.09375
- b_first: float32 [4096], P('narrow'), may hold values from -4 to 4
- w_second: bfloat16 [4096, 4096], P('narrow'), may hold values from -0.09375 to 0.09375
- b_second: float32 [4096], P('narrow'), may hold values from -4 to 4
- w_out: bfloat16 [4096], P('narrow'), may hold values from -0.09375 to 0.09375
Outputs:
- top_hidden: bfloat16 [16384, 4096], P('wide', 'narrow')
- logits: float32 [16384], P('wide')
- cache_next: bfloat16 [32, 8192, 128], P('wide', 'narrow')
The draws below stay inside these ranges and needn't reach their ends.
Inputs may be any that keep to these rules, and one draw needn't show every extreme that they name: `holder_counts`: entry h * 4 + o is the number of row blocks that holder h sections for owner o, the device holding slots o * 2048 to (o + 1) * 2048 - 1; a holder's counts sum to at most 1024, and this is reached by some holder of every table; the largest count, 512, is reached in every table. `miss_slots`: A holder's live entries are packed by owner, owner 0 first, as its counts say; each live entry names a slot of its owner, no slot twice in a table; entries past a holder's live ones are 0 and unused.
All inputs are finite; a program needn't handle non-finite values.
Results may differ from the reference program's by a relative error of at most 0.0076.
Values may be sent and summed in bfloat16 or wider, within the bound.
A program may use at most 128 MiB of HBM per device.

```python
import math
import jax
import jax.numpy as jnp
import numpy as np
from jax import lax

EMB = 128
HID = 4096
BAG = 16
SLOT_DEV = 2048
SEND_CAP = 512
HOLD_CAP = 1024
F = 32
BATCH = 16384
SLOTS = 8192
N_NARROW = 4


def miss_plan(key):
    holder_count = N_NARROW
    keys = [jax.random.fold_in(key, 9100 + number) for number in range(4)]
    share = SEND_CAP // (holder_count - 1)
    excess = SEND_CAP - share * (holder_count - 1)
    owners = jnp.arange(holder_count, dtype=jnp.int32)[None, None, :]
    holders = jnp.arange(holder_count, dtype=jnp.int32)[None, :, None]
    base = jax.random.randint(keys[0], (F, holder_count, holder_count), 0, share + 1, dtype=jnp.int32)
    hottest = jax.random.randint(keys[1], (F, 1, 1), 0, holder_count, dtype=jnp.int32)
    fullest = jax.random.randint(keys[2], (F, 1, 1), 0, holder_count, dtype=jnp.int32)
    counts = jnp.where(owners == hottest, SEND_CAP, base)
    ranking = owners - (owners > hottest).astype(jnp.int32)
    filled = jnp.where(owners == hottest, SEND_CAP, share + jnp.where(ranking == 0, excess, 0))
    counts = jnp.where(holders == fullest, filled, counts).astype(jnp.int32)
    before = jnp.cumsum(counts, axis=1) - counts
    starts = jnp.cumsum(counts, axis=2) - counts
    totals = jnp.sum(counts, axis=2)
    bound = max(1, 2 ** 30 // SLOT_DEV)
    scores = jax.random.randint(keys[3], (F, holder_count, SLOT_DEV), 0, bound, dtype=jnp.int32) * SLOT_DEV
    scores = scores + jnp.arange(SLOT_DEV, dtype=jnp.int32)[None, None, :]
    orders = jnp.argsort(scores, axis=-1, stable=True).astype(jnp.int32)
    places = jnp.arange(HOLD_CAP, dtype=jnp.int32)[None, None, :]
    endings = starts + counts
    owner_of = jnp.sum((places[:, :, :, None] >= endings[:, :, None, :]).astype(jnp.int32), axis=3)
    owner_of = jnp.minimum(owner_of, holder_count - 1)
    first_place = jnp.take_along_axis(starts, owner_of, axis=2)
    offsets = jnp.take_along_axis(before, owner_of, axis=2)
    live = places < totals[:, :, None]
    columns = jnp.where(live, offsets + places - first_place, 0)
    columns = jnp.clip(columns, 0, SLOT_DEV - 1)
    flat_index = (owner_of * SLOT_DEV + columns).reshape(F, holder_count * HOLD_CAP)
    picked = jnp.take_along_axis(orders.reshape(F, holder_count * SLOT_DEV), flat_index, axis=1)
    slots = jnp.where(live, owner_of * SLOT_DEV + picked.reshape(F, holder_count, HOLD_CAP), 0)
    return (counts.reshape(F, holder_count * holder_count), slots.reshape(F, holder_count * HOLD_CAP).astype(jnp.int32))


def draw_holder_counts(key, part):
    return miss_plan(key)[0]


def draw_miss_slots(key, part):
    return miss_plan(key)[1]


def place_ends(values, key, smallest, high):
    place = [jax.random.randint(jax.random.fold_in(key, axis), (), 0, length) for axis, length in enumerate(values.shape)]
    longest = values.shape.index(max(values.shape))
    neighbour = place[:longest] + [(place[longest] + 1) % values.shape[longest]] + place[longest + 1:]
    return values.at[tuple(place)].set(smallest).at[tuple(neighbour)].set(high)


def shard_levels(key, extent, split, low, largest):
    level, own = 1.0, jax.random.fold_in(key, 6)
    for axis_at, shards_of in split:
        draws = jnp.exp(jax.random.uniform(jax.random.fold_in(own, axis_at), (shards_of,), jnp.float32, low / len(split), largest / len(split)))
        level = level * jnp.repeat(draws, extent[axis_at] // shards_of).reshape([-1 if axis == axis_at else 1 for axis in range(len(extent))])
    return level


def rank_bounds(amount, lean):
    loads = [(1 << 20) // math.isqrt(grade ** lean) + 1 for grade in range(1, amount + 1)]
    deviation = 1 + sum(loads) // (1 << 30)
    return np.cumsum(np.array([max(1, weight // deviation) for weight in loads]))


def skewed_ids(rng, extent, count, slope):
    listing = rank_bounds(count, slope)
    ticket = jax.random.randint(jax.random.fold_in(rng, 1), extent, 0, int(listing[count - 1]))
    grade = jnp.searchsorted(jnp.asarray(listing, jnp.int32), ticket, side="right")
    return jax.random.permutation(jax.random.fold_in(rng, 2), count)[grade].astype(jnp.int32)


def noise(rng, dims, deviation, limit, split=(), kind=jnp.bfloat16):
    loudness = shard_levels(rng, dims, split, -0.22, 0.18) if split else 1.0
    entries = jax.random.normal(rng, dims, jnp.float32) * deviation * loudness
    return jnp.minimum(jnp.maximum(entries, -limit), limit).astype(kind)


def setup_inputs(seed: int = 0) -> dict:
    seeds = jax.random.split(jax.random.key(seed), 12)
    return {
        "cache": noise(seeds[0], (F, SLOTS, EMB), 1.0, 6.0, ((0, 32), (1, 4))),
        "lookup_slots": place_ends(skewed_ids(seeds[1], (F, BATCH, BAG), SLOTS, 2), jax.random.fold_in(seeds[1], 3), 0, SLOTS - 1).astype(jnp.int32),
        "bag_lengths": place_ends(jax.random.randint(seeds[2], (F, BATCH), 1, BAG + 1), jax.random.fold_in(seeds[2], 1), 1, BAG).astype(jnp.int32),
        "miss_rows": noise(seeds[3], (F, N_NARROW * HOLD_CAP, EMB), 1.0, 6.0, ((0, 32), (1, 4))),
        "miss_slots": draw_miss_slots(jax.random.fold_in(seeds[11], 71), 0),
        "holder_counts": draw_holder_counts(jax.random.fold_in(seeds[11], 71), 0),
        "w_first": noise(seeds[6], (F * EMB, HID), (F * EMB) ** -0.5, 0.09375, ((1, 4),)),
        "b_first": noise(seeds[7], (HID,), 1.0, 4.0, ((0, 4),), jnp.float32),
        "w_second": noise(seeds[8], (HID, HID), HID ** -0.5, 0.09375, ((0, 4),)),
        "b_second": noise(seeds[9], (HID,), 1.0, 4.0, ((0, 4),), jnp.float32),
        "w_out": noise(seeds[10], (HID,), HID ** -0.5, 0.09375, ((0, 4),)),
    }


def reference(cache, lookup_slots, bag_lengths, miss_rows, miss_slots, holder_counts, w_first, b_first, w_second, b_second, w_out):
    table_count, batch_rows, bag_size = lookup_slots.shape
    emb_width = cache.shape[2]
    block_rows = math.gcd(batch_rows, 2048)
    block_count = batch_rows // block_rows
    usable = jnp.arange(bag_size, dtype=jnp.int32)[None, None, :] < bag_lengths[:, :, None]
    slot_blocks = lookup_slots.reshape(table_count * block_count, block_rows, bag_size)
    usable_blocks = usable.reshape(table_count * block_count, block_rows, bag_size)
    table_ids = jnp.repeat(jnp.arange(table_count, dtype=jnp.int32), block_count)

    def pool_block(member):
        table_id, positions, keep = member
        chosen = lax.dynamic_index_in_dim(cache, table_id, 0, keepdims=False)
        gathered = jnp.take(chosen, positions, axis=0).astype(jnp.float32)
        return jnp.sum(jnp.where(keep[..., None], gathered, jnp.zeros((), jnp.float32)), axis=1)

    pooled = lax.map(pool_block, (table_ids, slot_blocks, usable_blocks))
    pooled = pooled.reshape(table_count, batch_rows, emb_width).astype(jnp.bfloat16)
    features = jnp.transpose(pooled, (1, 0, 2)).reshape(batch_rows, table_count * emb_width)
    first_hidden = jnp.maximum(jnp.dot(features, w_first, preferred_element_type=jnp.float32) + b_first, 0.0).astype(jnp.bfloat16)
    top_hidden = jnp.maximum(jnp.dot(first_hidden, w_second, preferred_element_type=jnp.float32) + b_second, 0.0).astype(jnp.bfloat16)
    logits = jnp.dot(top_hidden, w_out, preferred_element_type=jnp.float32)

    holder_count = N_NARROW
    hold_rows = HOLD_CAP
    counts = holder_counts.reshape(table_count, holder_count, holder_count)
    totals = jnp.sum(counts, axis=2)
    live = jnp.arange(hold_rows, dtype=jnp.int32)[None, None, :] < totals[:, :, None]
    targets = jnp.where(live, miss_slots.reshape(table_count, holder_count, hold_rows), cache.shape[1])
    targets = targets.reshape(table_count, holder_count * hold_rows).astype(jnp.int32)

    def refill(chosen, target_rows, sectioned):
        return chosen.at[target_rows].set(sectioned, mode="drop")

    cache_next = jax.vmap(refill)(cache, targets, miss_rows)
    return top_hidden, logits, cache_next
```

```python
import functools

import jax
import jax.numpy as jnp
from jax import lax
from jax.experimental import pallas as pl
from jax.experimental.pallas import tpu as pltpu
from jax.sharding import PartitionSpec as P

CHUNKS = 1
PAD = 16
UNROLL = 16
OWNERS_A_STEP = 4


def copy_for_each(x, axis):
    length = lax.axis_size(axis)
    return lax.all_to_all(jnp.broadcast_to(x[None], (length, *x.shape)), axis, 0, 0, tiled=True)


def pool_kernel(bag_size, rows, first, count, owners, index_ref, table_ref, out_ref, wide_ref, sum_ref):
    slots = table_ref.shape[0]

    @pl.when(pl.program_id(0) == 0)
    def _():
        wide_ref[:slots, :] = table_ref[...].astype(jnp.float32)
        wide_ref[slots:, :] = jnp.zeros((PAD, table_ref.shape[1]), jnp.float32)

    per_owner = count // UNROLL

    def step(i, _):
        owner = i // per_owner
        row = (i % per_owner) * UNROLL
        base = owner * (bag_size * rows) + first + row
        for u in range(UNROLL):
            terms = [
                wide_ref[pl.ds(index_ref[base + (l * rows + u)], 1), :] for l in range(bag_size)
            ]
            while len(terms) > 1:
                terms = [terms[k] + terms[k + 1] for k in range(0, len(terms), 2)]
            sum_ref[pl.ds(owner * count + row + u, 1), :] = terms[0]
        return 0

    lax.fori_loop(0, owners * per_owner, step, 0)
    out_ref[...] = sum_ref[...].astype(out_ref.dtype)


def pool_rows(table, indices, bag_size, rows, first, count):
    owner_count = indices.shape[0] // (bag_size * rows)
    owners = OWNERS_A_STEP
    slots, width = table.shape
    return pl.pallas_call(
        functools.partial(pool_kernel, bag_size, rows, first, count, owners),
        out_shape=jax.ShapeDtypeStruct((owner_count * count, width), jnp.bfloat16),
        grid=(owner_count // owners,),
        in_specs=[
            pl.BlockSpec((owners * bag_size * rows,), lambda i: (i,), memory_space=pltpu.SMEM),
            pl.BlockSpec((slots, width), lambda i: (0, 0), pipeline_mode=pl.Buffered(1)),
        ],
        out_specs=pl.BlockSpec((owners * count, width), lambda i: (i, 0)),
        scratch_shapes=[
            pltpu.VMEM((slots + PAD, width), jnp.float32),
            pltpu.VMEM((owners * count, width), jnp.float32),
        ],
        compiler_params=pltpu.CompilerParams(vmem_limit_bytes=16 << 20),
        cost_estimate=pl.CostEstimate(
            flops=2 * owner_count * count * bag_size * width * 400,
            bytes_accessed=slots * width * 2,
            transcendentals=0,
        ),
        name="pool",
    )(indices, table)


def body(
    cache,
    lookup_slots,
    bag_lengths,
    miss_rows,
    miss_slots,
    holder_counts,
    w_first,
    b_first,
    w_second,
    b_second,
    w_out,
):
    wide_count = lax.axis_size("wide")
    narrow_count = lax.axis_size("narrow")
    position = lax.axis_index("narrow")
    cache_table = cache[0]
    slot_count, width = cache_table.shape
    batch_rows, bag_size = lookup_slots.shape[1:]
    owner_rows = batch_rows // wide_count
    rows = owner_rows // narrow_count

    whole_table = copy_for_each(cache_table, "narrow").reshape(narrow_count * slot_count, width)

    by_lookup = lookup_slots[0].T.reshape(bag_size, wide_count, narrow_count, rows)
    by_lookup = lax.dynamic_index_in_dim(by_lookup, position, 2, keepdims=False)
    lengths = bag_lengths[0].reshape(wide_count, narrow_count, rows)
    lengths = lax.dynamic_index_in_dim(lengths, position, 1, keepdims=False)
    used = jnp.arange(bag_size, dtype=jnp.int32)[:, None, None] < lengths[None]
    indices = jnp.where(used, by_lookup, narrow_count * slot_count)
    indices = indices.transpose(1, 0, 2).reshape(wide_count * bag_size * rows)

    count = rows // CHUNKS
    first_slab = w_first.reshape(wide_count, width, w_first.shape[1])
    tops, logit_terms = [], []
    for chunk in range(CHUNKS):
        pooled = pool_rows(whole_table, indices, bag_size, rows, chunk * count, count)
        pooled = pooled.reshape(wide_count, count, width)
        arrived = lax.all_to_all(pooled, "wide", split_axis=0, concat_axis=0, tiled=True)
        features = lax.all_gather(arrived, "narrow", axis=1, tiled=True)
        first_terms = jnp.einsum(
            "fbe,feh->bh", features, first_slab, preferred_element_type=jnp.float32
        )
        first_hidden = jnp.maximum(first_terms + b_first, 0.0).astype(jnp.bfloat16)
        second_terms = jnp.dot(first_hidden, w_second, preferred_element_type=jnp.float32)
        second_summed = lax.psum_scatter(
            second_terms.astype(jnp.bfloat16), "narrow", scatter_dimension=1, tiled=True
        ).astype(jnp.float32)
        top = jnp.maximum(second_summed + b_second, 0.0).astype(jnp.bfloat16)
        logit_terms.append(jnp.dot(top, w_out, preferred_element_type=jnp.float32).reshape(narrow_count, count))
        tops.append(top.reshape(narrow_count, count, top.shape[1]))
    top_hidden = jnp.stack(tops, axis=1).reshape(owner_rows, tops[0].shape[2])
    logit_term = jnp.stack(logit_terms, axis=1).reshape(owner_rows)
    logits = jnp.sum(copy_for_each(logit_term, "narrow"), axis=0)

    total = jnp.sum(holder_counts[0])
    hold_rows = miss_slots.shape[1]
    live = jnp.arange(hold_rows, dtype=jnp.int32) < total
    held_slots = jnp.where(live, miss_slots[0], -1)
    all_slots = copy_for_each(held_slots, "narrow").reshape(narrow_count * hold_rows)
    all_rows = copy_for_each(miss_rows[0], "narrow").reshape(narrow_count * hold_rows, width)
    targets = all_slots - position * slot_count
    placing = targets[None, :] == jnp.arange(slot_count, dtype=jnp.int32)[:, None]
    placed = jnp.dot(
        placing.astype(jnp.bfloat16), all_rows, preferred_element_type=jnp.float32
    )
    struck = jnp.any(placing, axis=1)
    cache_next = jnp.where(struck[:, None], placed.astype(jnp.bfloat16), cache_table)[None]
    return (top_hidden, logits, cache_next)


def solution(mesh):
    return jax.shard_map(
        body,
        mesh=mesh,
        in_specs=(
            P("wide", "narrow", None),
            P("wide", None, None),
            P("wide", None),
            P("wide", "narrow", None),
            P("wide", "narrow"),
            P("wide", "narrow"),
            P(None, "narrow"),
            P("narrow"),
            P("narrow", None),
            P("narrow"),
            P("narrow"),
        ),
        out_specs=(P("wide", "narrow"), P("wide"), P("wide", "narrow", None)),
        check_vma=False,
    )
```

```python
import functools

import jax
import jax.numpy as jnp
from jax import lax
from jax.experimental import pallas as pl
from jax.experimental.pallas import tpu as pltpu
from jax.sharding import PartitionSpec as P

CHUNKS = 4
PAD = 16
UNROLL = 16
TILE = 256
MESH = pl.DeviceIdType.MESH


def copy_for_each(x, axis):
    length = lax.axis_size(axis)
    return lax.all_to_all(jnp.broadcast_to(x[None], (length, *x.shape)), axis, 0, 0, tiled=True)


def top_kernel(
    bag_size,
    wide_count,
    index_ref,
    cache_ref,
    w_first_hbm,
    b_first_ref,
    w_second_hbm,
    b_second_ref,
    top_ref,
    table,
    wide_table,
    pooled,
    sums,
    features,
    hidden,
    w_first,
    w_second,
    own_part,
    right_part,
    left_part,
    far_out,
    far_in,
    near_out,
    near_in,
    weight_sem,
    table_send,
    table_recv,
    exchange_send,
    exchange_recv,
    gather_send,
    gather_recv,
    pass_send,
    pass_recv,
    far_send,
    far_recv,
    near_send,
    near_recv,
):
    me = lax.axis_index("wide")
    place = lax.axis_index("narrow")
    right, left = lax.rem(place + 1, 4), lax.rem(place + 3, 4)
    slots, width = cache_ref.shape
    chunks, block, _ = features.shape
    rows = pooled.shape[1]
    count = rows // chunks
    owner_rows = top_ref.shape[0] // 4
    sides = ((0, right), (1, left))

    first_copy = pltpu.make_async_copy(w_first_hbm, w_first, weight_sem.at[0])
    second_copy = pltpu.make_async_copy(w_second_hbm, w_second, weight_sem.at[1])
    first_copy.start()
    second_copy.start()

    barrier = pltpu.get_barrier_semaphore()

    def greet(i, _):
        pl.semaphore_signal(
            barrier, inc=1, device_id={"wide": lax.rem(me + i, wide_count)}, device_id_type=MESH
        )
        return 0

    lax.fori_loop(1, wide_count, greet, 0)
    for _, other in sides:
        pl.semaphore_signal(barrier, inc=1, device_id={"narrow": other}, device_id_type=MESH)
    pl.semaphore_wait(barrier, wide_count + 1)

    def to_side(source, target, send, recv, other):
        return pltpu.make_async_remote_copy(
            src_ref=source,
            dst_ref=target,
            send_sem=send,
            recv_sem=recv,
            device_id={"narrow": other},
            device_id_type=MESH,
        )

    half = slots // 2
    near_tables = [
        to_side(cache_ref, table.at[place], table_send.at[k], table_recv.at[k], other)
        for k, other in sides
    ]
    for copy in near_tables:
        copy.start()
    wide_table[pl.ds(pl.multiple_of(place * slots, slots), slots), :] = cache_ref[...].astype(jnp.float32)
    wide_table[4 * slots :, :] = jnp.zeros((PAD, width), jnp.float32)
    far_tables = []
    for k, other, source in ((0, right, left), (1, left, right)):
        near_tables[k].wait_recv()
        part = table.at[source, pl.ds(k * half, half)]
        copy = to_side(part, part, table_send.at[2 + k], table_recv.at[2 + k], other)
        copy.start()
        far_tables.append(copy)

    def widen(source):
        wide_table[pl.ds(pl.multiple_of(source * slots, slots), slots), :] = table[source].astype(jnp.float32)

    widen(left)
    widen(right)
    for copy in far_tables:
        copy.wait_recv()
    widen(lax.rem(place + 2, 4))
    for copy in near_tables + far_tables:
        copy.wait_send()

    def pool(chunk, low, high):
        def owner_step(i, _):
            owner = lax.rem(me + i, wide_count)
            base = owner * (bag_size * rows) + chunk * count

            def row_step(j, _):
                for u in range(UNROLL):
                    terms = [
                        wide_table[pl.ds(index_ref[base + j * UNROLL + (l * rows + u)], 1), :]
                        for l in range(bag_size)
                    ]
                    while len(terms) > 1:
                        terms = [terms[k] + terms[k + 1] for k in range(0, len(terms), 2)]
                    sums[pl.ds(j * UNROLL + u, 1), :] = terms[0]
                return 0

            lax.fori_loop(0, count // UNROLL, row_step, 0)
            source = pooled.at[owner, pl.ds(chunk * count, count)]
            source[...] = sums[...].astype(jnp.bfloat16)
            target = features.at[
                chunk,
                pl.ds(pl.multiple_of(place * count, count), count),
                pl.ds(pl.multiple_of(me * width, width), width),
            ]

            @pl.when(i == 0)
            def _():
                pltpu.make_async_copy(source, target, exchange_recv.at[chunk]).start()

            @pl.when(i > 0)
            def _():
                pltpu.make_async_remote_copy(
                    src_ref=source,
                    dst_ref=target,
                    send_sem=exchange_send.at[chunk],
                    recv_sem=exchange_recv.at[chunk],
                    device_id={"wide": owner},
                    device_id_type=MESH,
                ).start()

            return 0

        lax.fori_loop(low, high, owner_step, 0)

    def own_rows(chunk, source, low, length):
        return features.at[chunk, pl.ds(pl.multiple_of(source * count + low, 16), length)]

    def near_copies(chunk):
        part = own_rows(chunk, place, 0, count)
        return [
            to_side(part, part, gather_send.at[chunk, k], gather_recv.at[chunk, k], other)
            for k, other in sides
        ]

    def pass_copies(chunk):
        part = count // 2
        found = []
        for k, other, source in ((0, right, left), (1, left, right)):
            view = own_rows(chunk, source, k * part, part)
            found.append(to_side(view, view, pass_send.at[chunk, k], pass_recv.at[chunk, k], other))
        return found

    def far_copies(chunk):
        return [
            to_side(far_out.at[chunk, k], far_in.at[chunk, k], far_send.at[chunk, k], far_recv.at[chunk, k], other)
            for k, other in sides
        ]

    def near_sums(chunk):
        return [
            to_side(near_out.at[chunk, k], near_in.at[chunk, k], near_send.at[chunk, k], near_recv.at[chunk, k], other)
            for k, other in sides
        ]

    def exchanged(chunk):
        whole = own_rows(chunk, place, 0, count)
        pltpu.make_async_copy(whole, whole, exchange_recv.at[chunk]).wait()
        for copy in near_copies(chunk):
            copy.start()

    def pass_on(chunk):
        for near, on in zip(near_copies(chunk), pass_copies(chunk)):
            near.wait_recv()
            on.start()

    middle = block // 2
    columns = top_ref.shape[1]

    def layers(chunk):
        for copy in pass_copies(chunk):
            copy.wait_recv()
        if chunk == 0:
            first_copy.wait()
            second_copy.wait()

        def first(t, _):
            span = pl.ds(pl.multiple_of(t * TILE, TILE), TILE)
            terms = jnp.dot(features[chunk], w_first[:, span], preferred_element_type=jnp.float32)
            hidden[:, span] = jnp.maximum(terms + b_first_ref[:, span], 0.0).astype(jnp.bfloat16)
            return 0

        lax.fori_loop(0, columns // TILE, first, 0)

        def second(ahead, keep):
            target = lax.rem(place + ahead, 4)

            def step(t, _):
                span = pl.ds(pl.multiple_of(t * TILE, TILE), TILE)
                from_ = pl.ds(pl.multiple_of(target * columns + t * TILE, TILE), TILE)
                keep(span, jnp.dot(hidden[...], w_second[:, from_], preferred_element_type=jnp.float32))
                return 0

            lax.fori_loop(0, columns // TILE, step, 0)

        def keep_far(span, terms):
            far_out[chunk, 0, :, span] = terms[:middle].astype(jnp.bfloat16)
            far_out[chunk, 1, :, span] = terms[middle:].astype(jnp.bfloat16)

        second(2, keep_far)
        for copy in far_copies(chunk):
            copy.start()

        def keep_right(span, terms):
            right_part[:, span] = terms

        def keep_left(span, terms):
            left_part[:, span] = terms

        def keep_own(span, terms):
            own_part[chunk, :, span] = terms

        second(1, keep_right)
        second(3, keep_left)
        second(0, keep_own)

    def join(chunk):
        parts = (right_part, left_part)
        for k, copy in enumerate(far_copies(chunk)):
            copy.wait_recv()
            summed = pl.ds(k * middle, middle)
            alone = pl.ds((1 - k) * middle, middle)
            near_out[chunk, k, summed, :] = (
                parts[k][summed, :] + far_in[chunk, k].astype(jnp.float32)
            ).astype(jnp.bfloat16)
            near_out[chunk, k, alone, :] = parts[k][alone, :].astype(jnp.bfloat16)
        for copy in near_sums(chunk):
            copy.start()

    def finish(chunk):
        for copy in near_sums(chunk):
            copy.wait_recv()
        terms = own_part[chunk] + near_in[chunk, 0].astype(jnp.float32) + near_in[chunk, 1].astype(jnp.float32)
        top = jnp.maximum(terms + b_second_ref[...], 0.0).astype(jnp.bfloat16)
        for q in range(4):
            top_ref[pl.ds(q * owner_rows + chunk * count, count), :] = top[q * count : (q + 1) * count]

    part = wide_count // 2
    for chunk in range(chunks + 1):
        for half_step in range(2):
            if chunk < chunks:
                pool(chunk, half_step * part, (half_step + 1) * part)
            if half_step == 0:
                if chunk >= 1:
                    exchanged(chunk - 1)
                if chunk >= 2:
                    layers(chunk - 2)
            else:
                if chunk >= 1:
                    pass_on(chunk - 1)
                if chunk >= 2:
                    join(chunk - 2)
                if chunk >= 3:
                    finish(chunk - 3)
    layers(chunks - 1)
    if chunks >= 2:
        finish(chunks - 2)
    join(chunks - 1)
    finish(chunks - 1)

    for chunk in range(chunks):
        sent = pooled.at[pl.ds(0, wide_count - 1), pl.ds(0, count)]
        pltpu.make_async_copy(sent, sent, exchange_send.at[chunk]).wait()
        for copies in (near_copies, pass_copies, far_copies, near_sums):
            for copy in copies(chunk):
                copy.wait_send()


def top_network(indices, cache_table, w_first, b_first, w_second, b_second, bag_size, wide_count):
    slots, width = cache_table.shape
    rows = indices.shape[0] // (bag_size * wide_count)
    count = rows // CHUNKS
    block = 4 * count
    fan_in, columns = w_first.shape
    vmem = pl.BlockSpec(memory_space=pltpu.VMEM)
    hbm = pl.BlockSpec(memory_space=pl.ANY)
    pairs = [pltpu.SemaphoreType.DMA((CHUNKS, 2))] * 8
    return pl.pallas_call(
        functools.partial(top_kernel, bag_size, wide_count),
        out_shape=jax.ShapeDtypeStruct((4 * rows, columns), jnp.bfloat16),
        in_specs=[pl.BlockSpec(memory_space=pltpu.SMEM), vmem, hbm, vmem, hbm, vmem],
        out_specs=vmem,
        scratch_shapes=[
            pltpu.VMEM((4, slots, width), jnp.bfloat16),
            pltpu.VMEM((4 * slots + PAD, width), jnp.float32),
            pltpu.VMEM((wide_count, rows, width), jnp.bfloat16),
            pltpu.VMEM((count, width), jnp.float32),
            pltpu.VMEM((CHUNKS, block, fan_in), jnp.bfloat16),
            pltpu.VMEM((block, columns), jnp.bfloat16),
            pltpu.VMEM((fan_in, columns), jnp.bfloat16),
            pltpu.VMEM((columns, fan_in), jnp.bfloat16),
            pltpu.VMEM((CHUNKS, block, columns), jnp.float32),
            pltpu.VMEM((block, columns), jnp.float32),
            pltpu.VMEM((block, columns), jnp.float32),
            pltpu.VMEM((CHUNKS, 2, block // 2, columns), jnp.bfloat16),
            pltpu.VMEM((CHUNKS, 2, block // 2, columns), jnp.bfloat16),
            pltpu.VMEM((CHUNKS, 2, block, columns), jnp.bfloat16),
            pltpu.VMEM((CHUNKS, 2, block, columns), jnp.bfloat16),
            pltpu.SemaphoreType.DMA((2,)),
            pltpu.SemaphoreType.DMA((4,)),
            pltpu.SemaphoreType.DMA((4,)),
            pltpu.SemaphoreType.DMA((CHUNKS,)),
            pltpu.SemaphoreType.DMA((CHUNKS,)),
            *pairs,
        ],
        compiler_params=pltpu.CompilerParams(
            collective_id=1, has_side_effects=True, vmem_limit_bytes=56 << 20
        ),
        cost_estimate=pl.CostEstimate(
            flops=4 * 4 * rows * fan_in * columns,
            bytes_accessed=2 * 2 * fan_in * columns,
            transcendentals=0,
        ),
        name="top_network",
    )(indices, cache_table, w_first, b_first[None], w_second, b_second[None])


def body(
    cache,
    lookup_slots,
    bag_lengths,
    miss_rows,
    miss_slots,
    holder_counts,
    w_first,
    b_first,
    w_second,
    b_second,
    w_out,
):
    wide_count = lax.axis_size("wide")
    narrow_count = lax.axis_size("narrow")
    position = lax.axis_index("narrow")
    cache_table = cache[0]
    slot_count, width = cache_table.shape
    batch_rows, bag_size = lookup_slots.shape[1:]
    owner_rows = batch_rows // wide_count
    rows = owner_rows // narrow_count

    by_lookup = lookup_slots[0].T.reshape(bag_size, wide_count, narrow_count, rows)
    by_lookup = lax.dynamic_index_in_dim(by_lookup, position, 2, keepdims=False)
    lengths = bag_lengths[0].reshape(wide_count, narrow_count, rows)
    lengths = lax.dynamic_index_in_dim(lengths, position, 1, keepdims=False)
    used = jnp.arange(bag_size, dtype=jnp.int32)[:, None, None] < lengths[None]
    indices = jnp.where(used, by_lookup, narrow_count * slot_count)
    indices = indices.transpose(1, 0, 2).reshape(wide_count * bag_size * rows)

    top_hidden = top_network(
        indices, cache_table, w_first, b_first, w_second, b_second, bag_size, wide_count
    )
    logit_term = jnp.dot(top_hidden, w_out, preferred_element_type=jnp.float32)
    logits = jnp.sum(copy_for_each(logit_term, "narrow"), axis=0)

    total = jnp.sum(holder_counts[0])
    hold_rows = miss_slots.shape[1]
    live = jnp.arange(hold_rows, dtype=jnp.int32) < total
    held_slots = jnp.where(live, miss_slots[0], -1)
    all_slots = copy_for_each(held_slots, "narrow").reshape(narrow_count * hold_rows)
    all_rows = copy_for_each(miss_rows[0], "narrow").reshape(narrow_count * hold_rows, width)
    targets = all_slots - position * slot_count
    placing = targets[None, :] == jnp.arange(slot_count, dtype=jnp.int32)[:, None]
    placed = jnp.dot(
        placing.astype(jnp.bfloat16), all_rows, preferred_element_type=jnp.float32
    )
    struck = jnp.any(placing, axis=1)
    cache_next = jnp.where(struck[:, None], placed.astype(jnp.bfloat16), cache_table)[None]
    return (top_hidden, logits, cache_next)


def solution(mesh):
    return jax.shard_map(
        body,
        mesh=mesh,
        in_specs=(
            P("wide", "narrow", None),
            P("wide", None, None),
            P("wide", None),
            P("wide", "narrow", None),
            P("wide", "narrow"),
            P("wide", "narrow"),
            P(None, "narrow"),
            P("narrow"),
            P("narrow", None),
            P("narrow"),
            P("narrow"),
        ),
        out_specs=(P("wide", "narrow"), P("wide"), P("wide", "narrow", None)),
        check_vma=False,
    )
```

```python
import functools

import jax
import jax.numpy as jnp
from jax import lax
from jax.experimental import pallas as pl
from jax.experimental.pallas import tpu as pltpu
from jax.sharding import PartitionSpec as P

CHUNKS = 4
PAD = 16
UNROLL = 16
TILE = 256
MESH = pl.DeviceIdType.MESH


def top_kernel(
    bag_size,
    wide_count,
    index_ref,
    cache_ref,
    w_first_hbm,
    b_first_ref,
    w_second_hbm,
    b_second_ref,
    w_out_ref,
    miss_rows_ref,
    miss_slots_ref,
    counts_ref,
    top_ref,
    logits_ref,
    cache_next_ref,
    table,
    wide_table,
    pooled,
    sums,
    features,
    hidden,
    w_first,
    w_second,
    own_part,
    right_part,
    left_part,
    far_out,
    far_in,
    near_out,
    near_in,
    held_rows,
    held_slots,
    logit_parts,
    weight_sem,
    table_send,
    table_recv,
    exchange_send,
    exchange_recv,
    gather_send,
    gather_recv,
    pass_send,
    pass_recv,
    far_send,
    far_recv,
    near_send,
    near_recv,
    rows_send,
    rows_recv,
    slots_send,
    slots_recv,
    logit_send,
    logit_recv,
):
    me = lax.axis_index("wide")
    place = lax.axis_index("narrow")
    right, left = lax.rem(place + 1, 4), lax.rem(place + 3, 4)
    slots, width = cache_ref.shape
    chunks, block, _ = features.shape
    rows = pooled.shape[1]
    count = rows // chunks
    owner_rows = top_ref.shape[0] // 4
    sides = ((0, right), (1, left))
    opposite = lax.rem(place + 2, 4)
    everyone = ((0, right), (1, left), (2, opposite))

    first_copy = pltpu.make_async_copy(w_first_hbm, w_first, weight_sem.at[0])
    second_copy = pltpu.make_async_copy(w_second_hbm, w_second, weight_sem.at[1])
    first_copy.start()
    second_copy.start()

    barrier = pltpu.get_barrier_semaphore()

    def greet(i, _):
        pl.semaphore_signal(
            barrier, inc=1, device_id={"wide": lax.rem(me + i, wide_count)}, device_id_type=MESH
        )
        return 0

    lax.fori_loop(1, wide_count, greet, 0)
    for _, other in everyone:
        pl.semaphore_signal(barrier, inc=1, device_id={"narrow": other}, device_id_type=MESH)

    hold = miss_rows_ref.shape[0]
    total = counts_ref[0] + counts_ref[1] + counts_ref[2] + counts_ref[3]
    position = lax.broadcasted_iota(jnp.int32, (1, hold), 1)
    held_slots[place] = jnp.where(position < total, miss_slots_ref[...], -1)
    held_rows[:, :, width:] = jnp.ones((4, hold, width), jnp.bfloat16)
    held_rows[place, :, :width] = miss_rows_ref[...]

    pl.semaphore_wait(barrier, wide_count + 2)

    def to_side(source, target, send, recv, other):
        return pltpu.make_async_remote_copy(
            src_ref=source,
            dst_ref=target,
            send_sem=send,
            recv_sem=recv,
            device_id={"narrow": other},
            device_id_type=MESH,
        )

    half = slots // 2
    near_tables = [
        to_side(cache_ref, table.at[place], table_send.at[k], table_recv.at[k], other)
        for k, other in sides
    ]
    for copy in near_tables:
        copy.start()
    wide_table[pl.ds(pl.multiple_of(place * slots, slots), slots), :] = cache_ref[...].astype(jnp.float32)
    wide_table[4 * slots :, :] = jnp.zeros((PAD, width), jnp.float32)
    far_tables = []
    for k, other, source in ((0, right, left), (1, left, right)):
        near_tables[k].wait_recv()
        part = table.at[source, pl.ds(k * half, half)]
        copy = to_side(part, part, table_send.at[2 + k], table_recv.at[2 + k], other)
        copy.start()
        far_tables.append(copy)

    def widen(source):
        wide_table[pl.ds(pl.multiple_of(source * slots, slots), slots), :] = table[source].astype(jnp.float32)

    widen(left)
    widen(right)
    for copy in far_tables:
        copy.wait_recv()
    widen(opposite)

    slot_copies = [
        to_side(held_slots.at[place], held_slots.at[place], slots_send.at[k], slots_recv.at[k], other)
        for k, other in everyone
    ]
    own_held = held_rows.at[place, :, pl.ds(0, width)]
    near_held = [
        to_side(own_held, own_held, rows_send.at[k], rows_recv.at[k], other) for k, other in sides
    ]
    for copy in slot_copies + near_held:
        copy.start()
    far_held = []
    for k, other, source in ((0, right, left), (1, left, right)):
        part = held_rows.at[source, pl.ds(k * (hold // 2), hold // 2), pl.ds(0, width)]
        far_held.append(to_side(part, part, rows_send.at[2 + k], rows_recv.at[2 + k], other))

    def pass_held():
        for near, far in zip(near_held, far_held):
            near.wait_recv()
            far.start()

    def held_arrived():
        for copy in slot_copies + far_held:
            copy.wait_recv()

    def refill(low, high):
        def step(t, _):
            span = pl.ds(pl.multiple_of(t * TILE, TILE), TILE)
            slot = place * slots + t * TILE + lax.broadcasted_iota(jnp.int32, (TILE, hold), 0)
            placed = jnp.zeros((TILE, 2 * width), jnp.float32)
            for q in range(4):
                chosen = jnp.where(held_slots[q] == slot, 1.0, 0.0).astype(jnp.bfloat16)
                placed += jnp.dot(chosen, held_rows[q], preferred_element_type=jnp.float32)
            cache_next_ref[span, :] = jnp.where(
                placed[:, width:] > 0.5, placed[:, :width].astype(jnp.bfloat16), cache_ref[span, :]
            )
            return 0

        lax.fori_loop(low, high, step, 0)

    def pool(chunk, low, high):
        def owner_step(i, _):
            owner = lax.rem(me + i, wide_count)
            base = owner * (bag_size * rows) + chunk * count

            def row_step(j, _):
                for u in range(UNROLL):
                    terms = [
                        wide_table[pl.ds(index_ref[base + j * UNROLL + (l * rows + u)], 1), :]
                        for l in range(bag_size)
                    ]
                    while len(terms) > 1:
                        terms = [terms[k] + terms[k + 1] for k in range(0, len(terms), 2)]
                    sums[pl.ds(j * UNROLL + u, 1), :] = terms[0]
                return 0

            lax.fori_loop(0, count // UNROLL, row_step, 0)
            source = pooled.at[owner, pl.ds(chunk * count, count)]
            source[...] = sums[...].astype(jnp.bfloat16)
            target = features.at[
                chunk,
                pl.ds(pl.multiple_of(place * count, count), count),
                pl.ds(pl.multiple_of(me * width, width), width),
            ]

            @pl.when(i == 0)
            def _():
                pltpu.make_async_copy(source, target, exchange_recv.at[chunk]).start()

            @pl.when(i > 0)
            def _():
                pltpu.make_async_remote_copy(
                    src_ref=source,
                    dst_ref=target,
                    send_sem=exchange_send.at[chunk],
                    recv_sem=exchange_recv.at[chunk],
                    device_id={"wide": owner},
                    device_id_type=MESH,
                ).start()

            return 0

        lax.fori_loop(low, high, owner_step, 0)

    def own_rows(chunk, source, low, length):
        return features.at[chunk, pl.ds(pl.multiple_of(source * count + low, 16), length)]

    def near_copies(chunk):
        part = own_rows(chunk, place, 0, count)
        return [
            to_side(part, part, gather_send.at[chunk, k], gather_recv.at[chunk, k], other)
            for k, other in sides
        ]

    def pass_copies(chunk):
        part = count // 2
        found = []
        for k, other, source in ((0, right, left), (1, left, right)):
            view = own_rows(chunk, source, k * part, part)
            found.append(to_side(view, view, pass_send.at[chunk, k], pass_recv.at[chunk, k], other))
        return found

    def far_copies(chunk):
        return [
            to_side(far_out.at[chunk, k], far_in.at[chunk, k], far_send.at[chunk, k], far_recv.at[chunk, k], other)
            for k, other in sides
        ]

    def near_sums(chunk):
        return [
            to_side(near_out.at[chunk, k], near_in.at[chunk, k], near_send.at[chunk, k], near_recv.at[chunk, k], other)
            for k, other in sides
        ]

    def exchanged(chunk):
        whole = own_rows(chunk, place, 0, count)
        pltpu.make_async_copy(whole, whole, exchange_recv.at[chunk]).wait()
        for copy in near_copies(chunk):
            copy.start()

    def pass_on(chunk):
        for near, on in zip(near_copies(chunk), pass_copies(chunk)):
            near.wait_recv()
            on.start()

    middle = block // 2
    columns = top_ref.shape[1]

    def layers(chunk):
        for copy in pass_copies(chunk):
            copy.wait_recv()
        if chunk == 0:
            first_copy.wait()
            second_copy.wait()

        def first(t, _):
            span = pl.ds(pl.multiple_of(t * TILE, TILE), TILE)
            terms = jnp.dot(features[chunk], w_first[:, span], preferred_element_type=jnp.float32)
            hidden[:, span] = jnp.maximum(terms + b_first_ref[:, span], 0.0).astype(jnp.bfloat16)
            return 0

        lax.fori_loop(0, columns // TILE, first, 0)

        def second(ahead, keep):
            target = lax.rem(place + ahead, 4)

            def step(t, _):
                span = pl.ds(pl.multiple_of(t * TILE, TILE), TILE)
                from_ = pl.ds(pl.multiple_of(target * columns + t * TILE, TILE), TILE)
                keep(span, jnp.dot(hidden[...], w_second[:, from_], preferred_element_type=jnp.float32))
                return 0

            lax.fori_loop(0, columns // TILE, step, 0)

        def keep_far(span, terms):
            far_out[chunk, 0, :, span] = terms[:middle].astype(jnp.bfloat16)
            far_out[chunk, 1, :, span] = terms[middle:].astype(jnp.bfloat16)

        second(2, keep_far)
        for copy in far_copies(chunk):
            copy.start()

        def keep_right(span, terms):
            right_part[:, span] = terms

        def keep_left(span, terms):
            left_part[:, span] = terms

        def keep_own(span, terms):
            own_part[chunk, :, span] = terms

        second(1, keep_right)
        second(3, keep_left)
        second(0, keep_own)

    def join(chunk):
        parts = (right_part, left_part)
        for k, copy in enumerate(far_copies(chunk)):
            copy.wait_recv()
            summed = pl.ds(k * middle, middle)
            alone = pl.ds((1 - k) * middle, middle)
            near_out[chunk, k, summed, :] = (
                parts[k][summed, :] + far_in[chunk, k].astype(jnp.float32)
            ).astype(jnp.bfloat16)
            near_out[chunk, k, alone, :] = parts[k][alone, :].astype(jnp.bfloat16)
        for copy in near_sums(chunk):
            copy.start()

    def finish(chunk):
        for copy in near_sums(chunk):
            copy.wait_recv()
        terms = own_part[chunk] + near_in[chunk, 0].astype(jnp.float32) + near_in[chunk, 1].astype(jnp.float32)
        top = jnp.maximum(terms + b_second_ref[...], 0.0).astype(jnp.bfloat16)
        for q in range(4):
            top_ref[pl.ds(q * owner_rows + chunk * count, count), :] = top[q * count : (q + 1) * count]

    part = wide_count // 2
    blocks = slots // TILE
    for chunk in range(chunks + 1):
        for half_step in range(2):
            if chunk < chunks:
                pool(chunk, half_step * part, (half_step + 1) * part)
            if half_step == 0:
                if chunk == 0:
                    pass_held()
                if chunk >= 1:
                    exchanged(chunk - 1)
                if chunk >= 2:
                    layers(chunk - 2)
            else:
                if chunk == 0:
                    held_arrived()
                if chunk >= 1:
                    pass_on(chunk - 1)
                if chunk >= 2:
                    join(chunk - 2)
                if chunk >= 3:
                    finish(chunk - 3)
    refill(0, blocks // 2)
    layers(chunks - 1)
    finish(chunks - 2)
    join(chunks - 1)
    refill(blocks // 2, blocks)
    finish(chunks - 1)

    logit_parts[place] = lax.dot_general(
        w_out_ref[...], top_ref[...], (((1,), (1,)), ((), ())), preferred_element_type=jnp.float32
    )[:8]
    logit_copies = [
        to_side(logit_parts.at[place], logit_parts.at[place], logit_send.at[k], logit_recv.at[k], other)
        for k, other in everyone
    ]
    for copy in logit_copies:
        copy.start()
    for chunk in range(chunks):
        sent = pooled.at[pl.ds(0, wide_count - 1), pl.ds(0, count)]
        pltpu.make_async_copy(sent, sent, exchange_send.at[chunk]).wait()
        for copies in (near_copies, pass_copies, far_copies, near_sums):
            for copy in copies(chunk):
                copy.wait_send()
    for copy in near_tables + far_tables + slot_copies + near_held + far_held:
        copy.wait_send()
    for copy in logit_copies:
        copy.wait_recv()
    logits_ref[...] = (
        logit_parts[0][:1] + logit_parts[1][:1] + (logit_parts[2][:1] + logit_parts[3][:1])
    )
    for copy in logit_copies:
        copy.wait_send()


def top_network(
    indices,
    cache_table,
    w_first,
    b_first,
    w_second,
    b_second,
    w_out,
    miss_rows,
    miss_slots,
    counts,
    bag_size,
    wide_count,
):
    slots, width = cache_table.shape
    rows = indices.shape[0] // (bag_size * wide_count)
    count = rows // CHUNKS
    block = 4 * count
    fan_in, columns = w_first.shape
    vmem = pl.BlockSpec(memory_space=pltpu.VMEM)
    hbm = pl.BlockSpec(memory_space=pl.ANY)
    smem = pl.BlockSpec(memory_space=pltpu.SMEM)
    hold = miss_rows.shape[0]
    pairs = [pltpu.SemaphoreType.DMA((CHUNKS, 2))] * 8
    return pl.pallas_call(
        functools.partial(top_kernel, bag_size, wide_count),
        out_shape=(
            jax.ShapeDtypeStruct((4 * rows, columns), jnp.bfloat16),
            jax.ShapeDtypeStruct((1, 4 * rows), jnp.float32),
            jax.ShapeDtypeStruct((slots, width), jnp.bfloat16),
        ),
        in_specs=[smem, vmem, hbm, vmem, hbm, vmem, vmem, vmem, vmem, smem],
        out_specs=(vmem, vmem, vmem),
        scratch_shapes=[
            pltpu.VMEM((4, slots, width), jnp.bfloat16),
            pltpu.VMEM((4 * slots + PAD, width), jnp.float32),
            pltpu.VMEM((wide_count, rows, width), jnp.bfloat16),
            pltpu.VMEM((count, width), jnp.float32),
            pltpu.VMEM((CHUNKS, block, fan_in), jnp.bfloat16),
            pltpu.VMEM((block, columns), jnp.bfloat16),
            pltpu.VMEM((fan_in, columns), jnp.bfloat16),
            pltpu.VMEM((columns, fan_in), jnp.bfloat16),
            pltpu.VMEM((CHUNKS, block, columns), jnp.float32),
            pltpu.VMEM((block, columns), jnp.float32),
            pltpu.VMEM((block, columns), jnp.float32),
            pltpu.VMEM((CHUNKS, 2, block // 2, columns), jnp.bfloat16),
            pltpu.VMEM((CHUNKS, 2, block // 2, columns), jnp.bfloat16),
            pltpu.VMEM((CHUNKS, 2, block, columns), jnp.bfloat16),
            pltpu.VMEM((CHUNKS, 2, block, columns), jnp.bfloat16),
            pltpu.VMEM((4, hold, 2 * width), jnp.bfloat16),
            pltpu.VMEM((4, 1, hold), jnp.int32),
            pltpu.VMEM((4, 8, 4 * rows), jnp.float32),
            pltpu.SemaphoreType.DMA((2,)),
            pltpu.SemaphoreType.DMA((4,)),
            pltpu.SemaphoreType.DMA((4,)),
            pltpu.SemaphoreType.DMA((CHUNKS,)),
            pltpu.SemaphoreType.DMA((CHUNKS,)),
            *pairs,
            pltpu.SemaphoreType.DMA((4,)),
            pltpu.SemaphoreType.DMA((4,)),
            *[pltpu.SemaphoreType.DMA((3,))] * 4,
        ],
        compiler_params=pltpu.CompilerParams(
            collective_id=1, has_side_effects=True, vmem_limit_bytes=56 << 20
        ),
        cost_estimate=pl.CostEstimate(
            flops=4 * 4 * rows * fan_in * columns,
            bytes_accessed=2 * 2 * fan_in * columns,
            transcendentals=0,
        ),
        name="top_network",
    )(
        indices,
        cache_table,
        w_first,
        b_first[None],
        w_second,
        b_second[None],
        jnp.broadcast_to(w_out[None], (16, columns)),
        miss_rows,
        miss_slots,
        counts,
    )


def body(
    cache,
    lookup_slots,
    bag_lengths,
    miss_rows,
    miss_slots,
    holder_counts,
    w_first,
    b_first,
    w_second,
    b_second,
    w_out,
):
    wide_count = lax.axis_size("wide")
    narrow_count = lax.axis_size("narrow")
    position = lax.axis_index("narrow")
    cache_table = cache[0]
    slot_count, width = cache_table.shape
    batch_rows, bag_size = lookup_slots.shape[1:]
    owner_rows = batch_rows // wide_count
    rows = owner_rows // narrow_count

    by_lookup = lookup_slots[0].T.reshape(bag_size, wide_count, narrow_count, rows)
    by_lookup = lax.dynamic_index_in_dim(by_lookup, position, 2, keepdims=False)
    lengths = bag_lengths[0].reshape(wide_count, narrow_count, rows)
    lengths = lax.dynamic_index_in_dim(lengths, position, 1, keepdims=False)
    used = jnp.arange(bag_size, dtype=jnp.int32)[:, None, None] < lengths[None]
    indices = jnp.where(used, by_lookup, narrow_count * slot_count)
    indices = indices.transpose(1, 0, 2).reshape(wide_count * bag_size * rows)

    top_hidden, logits, cache_next = top_network(
        indices,
        cache_table,
        w_first,
        b_first,
        w_second,
        b_second,
        w_out,
        miss_rows[0],
        miss_slots,
        holder_counts[0],
        bag_size,
        wide_count,
    )
    return (top_hidden, logits[0], cache_next[None])


def solution(mesh):
    return jax.shard_map(
        body,
        mesh=mesh,
        in_specs=(
            P("wide", "narrow", None),
            P("wide", None, None),
            P("wide", None),
            P("wide", "narrow", None),
            P("wide", "narrow"),
            P("wide", "narrow"),
            P(None, "narrow"),
            P("narrow"),
            P("narrow", None),
            P("narrow"),
            P("narrow"),
        ),
        out_specs=(P("wide", "narrow"), P("wide"), P("wide", "narrow", None)),
        check_vma=False,
    )
```

```python
import jax
import jax.numpy as jnp
from jax import lax
from jax.experimental import pallas as pl
from jax.experimental.pallas import tpu as pltpu
from jax.sharding import PartitionSpec as P

COUNTS = (32, 32, 32, 32)
STEPS = 4
PAD = 16
UNROLL = 16
TILE = 256
MESH = pl.DeviceIdType.MESH


def top_kernel(
    lookups_hbm,
    lengths_hbm,
    cache_ref,
    w_first_hbm,
    b_first_ref,
    w_second_hbm,
    b_second_ref,
    w_out_ref,
    miss_rows_ref,
    miss_slots_ref,
    counts_ref,
    top_ref,
    logits_ref,
    cache_next_ref,
    lookups,
    lengths,
    index_ref,
    table,
    wide_table,
    pooled,
    sums,
    features,
    hidden,
    w_first,
    w_second,
    own_part,
    right_part,
    left_part,
    far_out,
    far_in,
    near_out,
    near_in,
    held_rows,
    held_slots,
    logit_parts,
    index_sem,
    weight_sem,
    table_send,
    table_recv,
    exchange_send,
    exchange_recv,
    gather_send,
    gather_recv,
    pass_send,
    pass_recv,
    far_send,
    far_recv,
    near_send,
    near_recv,
    rows_send,
    rows_recv,
    slots_send,
    slots_recv,
    logit_send,
    logit_recv,
):
    me = lax.axis_index("wide")
    place = lax.axis_index("narrow")
    right, left = lax.rem(place + 1, 4), lax.rem(place + 3, 4)
    slots, width = cache_ref.shape
    wide_count, rows, _ = pooled.shape
    bag_size = lookups.shape[1]
    owner_rows = 4 * rows
    chunks = len(COUNTS)
    starts = tuple(sum(COUNTS[:chunk]) for chunk in range(chunks))
    fan_in, columns = w_first.shape
    sides = ((0, right), (1, left))
    opposite = lax.rem(place + 2, 4)
    everyone = ((0, right), (1, left), (2, opposite))

    def own_span(owner):
        return pl.ds(pl.multiple_of((owner * 4 + place) * rows, rows), rows)

    def fetch(owner, _):
        pltpu.make_async_copy(lookups_hbm.at[:, own_span(owner)], lookups.at[owner], index_sem.at[0]).start()
        return 0

    lax.fori_loop(0, wide_count, fetch, 0)
    lengths_copy = pltpu.make_async_copy(lengths_hbm, lengths, index_sem.at[1])
    lengths_copy.start()
    first_copy = pltpu.make_async_copy(w_first_hbm, w_first, weight_sem.at[0])
    second_copy = pltpu.make_async_copy(w_second_hbm, w_second, weight_sem.at[1])
    first_copy.start()
    second_copy.start()

    barrier = pltpu.get_barrier_semaphore()

    def greet(i, _):
        pl.semaphore_signal(
            barrier, inc=1, device_id={"wide": lax.rem(me + i, wide_count)}, device_id_type=MESH
        )
        return 0

    lax.fori_loop(1, wide_count, greet, 0)
    for _, other in everyone:
        pl.semaphore_signal(barrier, inc=1, device_id={"narrow": other}, device_id_type=MESH)

    hold = miss_rows_ref.shape[0]
    total = counts_ref[0] + counts_ref[1] + counts_ref[2] + counts_ref[3]
    position = lax.broadcasted_iota(jnp.int32, (1, hold), 1)
    held_slots[place] = jnp.where(position < total, miss_slots_ref[...], -1)
    held_rows[:, :, width:] = jnp.ones((4, hold, width), jnp.bfloat16)
    held_rows[place, :, :width] = miss_rows_ref[...]

    pl.semaphore_wait(barrier, wide_count + 2)

    def to_side(source, target, send, recv, other):
        return pltpu.make_async_remote_copy(
            src_ref=source,
            dst_ref=target,
            send_sem=send,
            recv_sem=recv,
            device_id={"narrow": other},
            device_id_type=MESH,
        )

    half = slots // 2
    near_tables = []
    for late in range(2):
        for k, other in sides:
            span = pl.ds((late ^ k) * half, half)
            near_tables.append(
                to_side(
                    cache_ref.at[span],
                    table.at[place, span],
                    table_send.at[2 * late + k],
                    table_recv.at[2 * late + k],
                    other,
                )
            )
    for copy in near_tables:
        copy.start()
    wide_table[pl.ds(pl.multiple_of(place * slots, slots), slots), :] = cache_ref[...].astype(jnp.float32)
    wide_table[4 * slots :, :] = jnp.zeros((PAD, width), jnp.float32)

    pltpu.make_async_copy(lookups, lookups, index_sem.at[0]).wait()
    lengths_copy.wait()

    def mask(owner, _):
        number = lax.broadcasted_iota(jnp.int32, (bag_size, rows), 0)
        lookups[owner] = jnp.where(number < lengths[:, own_span(owner)], lookups[owner], 4 * slots)
        return 0

    lax.fori_loop(0, wide_count, mask, 0)
    index_copy = pltpu.make_async_copy(lookups, index_ref, index_sem.at[2])
    index_copy.start()
    far_tables = []
    for k, other, source in ((0, right, left), (1, left, right)):
        near_tables[k].wait_recv()
        part = table.at[source, pl.ds(k * half, half)]
        copy = to_side(part, part, table_send.at[4 + k], table_recv.at[4 + k], other)
        copy.start()
        far_tables.append(copy)

    def widen(source):
        wide_table[pl.ds(pl.multiple_of(source * slots, slots), slots), :] = table[source].astype(jnp.float32)

    for copy in near_tables[2:]:
        copy.wait_recv()
    widen(left)
    widen(right)
    for copy in far_tables:
        copy.wait_recv()
    widen(opposite)
    index_copy.wait()

    slot_copies = [
        to_side(held_slots.at[place], held_slots.at[place], slots_send.at[k], slots_recv.at[k], other)
        for k, other in everyone
    ]
    own_held = held_rows.at[place, :, pl.ds(0, width)]
    near_held = [
        to_side(own_held, own_held, rows_send.at[k], rows_recv.at[k], other) for k, other in sides
    ]
    for copy in slot_copies + near_held:
        copy.start()
    far_held = []
    for k, other, source in ((0, right, left), (1, left, right)):
        part = held_rows.at[source, pl.ds(k * (hold // 2), hold // 2), pl.ds(0, width)]
        far_held.append(to_side(part, part, rows_send.at[2 + k], rows_recv.at[2 + k], other))

    def pass_held():
        for near, far in zip(near_held, far_held):
            near.wait_recv()
            far.start()

    def held_arrived():
        for copy in slot_copies + far_held:
            copy.wait_recv()

    def refill(low, high):
        def step(t, _):
            span = pl.ds(pl.multiple_of(t * TILE, TILE), TILE)
            slot = place * slots + t * TILE + lax.broadcasted_iota(jnp.int32, (TILE, hold), 0)
            placed = jnp.zeros((TILE, 2 * width), jnp.float32)
            for q in range(4):
                chosen = jnp.where(held_slots[q] == slot, 1.0, 0.0).astype(jnp.bfloat16)
                placed += jnp.dot(chosen, held_rows[q], preferred_element_type=jnp.float32)
            cache_next_ref[span, :] = jnp.where(
                placed[:, width:] > 0.5, placed[:, :width].astype(jnp.bfloat16), cache_ref[span, :]
            )
            return 0

        lax.fori_loop(low, high, step, 0)

    def pool(chunk, low, high):
        count, start = COUNTS[chunk], starts[chunk]

        def owner_step(i, _):
            owner = lax.rem(me + i, wide_count)
            for row in range(0, count, UNROLL):
                for u in range(row, row + UNROLL):
                    terms = [
                        wide_table[pl.ds(index_ref[owner, l, start + u], 1), :] for l in range(bag_size)
                    ]
                    while len(terms) > 1:
                        terms = [terms[k] + terms[k + 1] for k in range(0, len(terms), 2)]
                    sums[pl.ds(u, 1), :] = terms[0]
            source = pooled.at[owner, pl.ds(start, count)]
            source[...] = sums[:count, :].astype(jnp.bfloat16)
            target = features.at[
                pl.ds(pl.multiple_of(4 * start + place * count, 16), count),
                pl.ds(pl.multiple_of(me * width, width), width),
            ]

            @pl.when(i == 0)
            def _():
                pltpu.make_async_copy(source, target, exchange_recv.at[chunk]).start()

            @pl.when(i > 0)
            def _():
                pltpu.make_async_remote_copy(
                    src_ref=source,
                    dst_ref=target,
                    send_sem=exchange_send.at[chunk],
                    recv_sem=exchange_recv.at[chunk],
                    device_id={"wide": owner},
                    device_id_type=MESH,
                ).start()

            return 0

        lax.fori_loop(low, high, owner_step, 0)

    def own_rows(chunk, source):
        return pl.ds(pl.multiple_of(4 * starts[chunk] + source * COUNTS[chunk], 16), COUNTS[chunk])

    def near_copies(chunk):
        part = features.at[own_rows(chunk, place)]
        return [
            to_side(part, part, gather_send.at[chunk, k], gather_recv.at[chunk, k], other)
            for k, other in sides
        ]

    def pass_copies(chunk):
        found = []
        for k, other, source in ((0, right, left), (1, left, right)):
            view = features.at[own_rows(chunk, source), pl.ds(k * (fan_in // 2), fan_in // 2)]
            found.append(to_side(view, view, pass_send.at[chunk, k], pass_recv.at[chunk, k], other))
        return found

    def far_copies(chunk):
        span = pl.ds(2 * starts[chunk], 2 * COUNTS[chunk])
        return [
            to_side(far_out.at[k, span], far_in.at[k, span], far_send.at[chunk, k], far_recv.at[chunk, k], other)
            for k, other in sides
        ]

    def near_sums(chunk):
        span = pl.ds(4 * starts[chunk], 4 * COUNTS[chunk])
        return [
            to_side(near_out.at[k, span], near_in.at[k, span], near_send.at[chunk, k], near_recv.at[chunk, k], other)
            for k, other in sides
        ]

    def exchanged(chunk):
        whole = features.at[own_rows(chunk, place)]
        pltpu.make_async_copy(whole, whole, exchange_recv.at[chunk]).wait()
        for copy in near_copies(chunk):
            copy.start()

    def pass_on(chunk):
        for near, on in zip(near_copies(chunk), pass_copies(chunk)):
            near.wait_recv()
            on.start()

    def layers(chunk):
        block, middle = 4 * COUNTS[chunk], 2 * COUNTS[chunk]
        begin = 4 * starts[chunk]
        for copy in pass_copies(chunk):
            copy.wait_recv()
        if chunk == 0:
            first_copy.wait()
            second_copy.wait()

        def first(t, _):
            span = pl.ds(pl.multiple_of(t * TILE, TILE), TILE)
            terms = jnp.dot(features[pl.ds(begin, block), :], w_first[:, span], preferred_element_type=jnp.float32)
            hidden[:block, span] = jnp.maximum(terms + b_first_ref[:, span], 0.0).astype(jnp.bfloat16)
            return 0

        lax.fori_loop(0, columns // TILE, first, 0, unroll=True)

        def second(ahead, keep):
            target = lax.rem(place + ahead, 4)

            def step(t, _):
                span = pl.ds(pl.multiple_of(t * TILE, TILE), TILE)
                from_ = pl.ds(pl.multiple_of(target * columns + t * TILE, TILE), TILE)
                keep(span, jnp.dot(hidden[:block, :], w_second[:, from_], preferred_element_type=jnp.float32))
                return 0

            lax.fori_loop(0, columns // TILE, step, 0, unroll=True)

        def keep_far(span, terms):
            for k in range(2):
                half_rows = terms[k * middle : (k + 1) * middle]
                far_out[k, pl.ds(2 * starts[chunk], middle), span] = half_rows.astype(jnp.bfloat16)

        second(2, keep_far)
        for copy in far_copies(chunk):
            copy.start()

        def keep_right(span, terms):
            right_part[:block, span] = terms

        def keep_left(span, terms):
            left_part[:block, span] = terms

        def keep_own(span, terms):
            own_part[pl.ds(begin, block), span] = terms

        second(1, keep_right)
        second(3, keep_left)
        second(0, keep_own)

    def join(chunk):
        middle, begin = 2 * COUNTS[chunk], 4 * starts[chunk]
        parts = (right_part, left_part)
        for k, copy in enumerate(far_copies(chunk)):
            copy.wait_recv()
            summed, alone = k * middle, (1 - k) * middle
            came = far_in[k, pl.ds(2 * starts[chunk], middle), :].astype(jnp.float32)
            near_out[k, pl.ds(begin + summed, middle), :] = (
                parts[k][pl.ds(summed, middle), :] + came
            ).astype(jnp.bfloat16)
            near_out[k, pl.ds(begin + alone, middle), :] = parts[k][pl.ds(alone, middle), :].astype(jnp.bfloat16)
        for copy in near_sums(chunk):
            copy.start()

    def finish(chunk):
        for copy in near_sums(chunk):
            copy.wait_recv()
        count = COUNTS[chunk]
        for q in range(4):
            span = pl.ds(4 * starts[chunk] + q * count, count)
            terms = own_part[span, :] + near_in[0, span, :].astype(jnp.float32) + near_in[1, span, :].astype(jnp.float32)
            top_ref[pl.ds(q * rows + starts[chunk], count), :] = jnp.maximum(
                terms + b_second_ref[...], 0.0
            ).astype(jnp.bfloat16)

    part = wide_count // STEPS
    blocks = slots // TILE
    for chunk in range(chunks):
        for step in range(STEPS):
            pool(chunk, step * part, (step + 1) * part)
            if chunk == 0 and step == 1:
                pass_held()
            if step == 0 and chunk >= 1:
                exchanged(chunk - 1)
            if step == 1 and chunk >= 2:
                layers(chunk - 2)
            if step == 2 and chunk >= 1:
                pass_on(chunk - 1)
            if step == 3 and chunk >= 2:
                join(chunk - 2)
            if step == 1 and chunk >= 3:
                finish(chunk - 3)
    last = chunks - 1
    exchanged(last)
    layers(last - 1)
    held_arrived()
    finish(last - 2)
    pass_on(last)
    refill(0, blocks // 2)
    join(last - 1)
    layers(last)
    refill(blocks // 2, blocks)
    join(last)
    finish(last - 1)
    finish(last)

    logit_parts[place] = lax.dot_general(
        jnp.broadcast_to(w_out_ref[...], (8, columns)).astype(jnp.bfloat16),
        top_ref[...],
        (((1,), (1,)), ((), ())),
        preferred_element_type=jnp.float32,
    )
    logit_copies = [
        to_side(logit_parts.at[place], logit_parts.at[place], logit_send.at[k], logit_recv.at[k], other)
        for k, other in everyone
    ]
    for copy in logit_copies:
        copy.start()
    for chunk in range(chunks):
        sent = pooled.at[pl.ds(0, wide_count - 1), pl.ds(0, COUNTS[chunk])]
        pltpu.make_async_copy(sent, sent, exchange_send.at[chunk]).wait()
        for copies in (near_copies, pass_copies, far_copies, near_sums):
            for copy in copies(chunk):
                copy.wait_send()
    for copy in near_tables + far_tables + slot_copies + near_held + far_held:
        copy.wait_send()
    for copy in logit_copies:
        copy.wait_recv()
    logits_ref[...] = (
        logit_parts[0][:1] + logit_parts[1][:1] + (logit_parts[2][:1] + logit_parts[3][:1])
    )
    for copy in logit_copies:
        copy.wait_send()


def top_network(
    lookups,
    lengths,
    cache_table,
    w_first,
    b_first,
    w_second,
    b_second,
    w_out,
    miss_rows,
    miss_slots,
    counts,
    wide_count,
):
    slots, width = cache_table.shape
    bag_size, batch_rows = lookups.shape
    rows = batch_rows // (4 * wide_count)
    chunks = len(COUNTS)
    block = 4 * max(COUNTS)
    fan_in, columns = w_first.shape
    vmem = pl.BlockSpec(memory_space=pltpu.VMEM)
    hbm = pl.BlockSpec(memory_space=pl.ANY)
    smem = pl.BlockSpec(memory_space=pltpu.SMEM)
    hold = miss_rows.shape[0]
    pairs = [pltpu.SemaphoreType.DMA((chunks, 2))] * 8
    return pl.pallas_call(
        top_kernel,
        out_shape=(
            jax.ShapeDtypeStruct((4 * rows, columns), jnp.bfloat16),
            jax.ShapeDtypeStruct((1, 4 * rows), jnp.float32),
            jax.ShapeDtypeStruct((slots, width), jnp.bfloat16),
        ),
        in_specs=[hbm, hbm, vmem, hbm, vmem, hbm, vmem, vmem, vmem, vmem, smem],
        out_specs=(vmem, vmem, vmem),
        scratch_shapes=[
            pltpu.VMEM((wide_count, bag_size, rows), jnp.int32),
            pltpu.VMEM((1, batch_rows), jnp.int32),
            pltpu.SMEM((wide_count, bag_size, rows), jnp.int32),
            pltpu.VMEM((4, slots, width), jnp.bfloat16),
            pltpu.VMEM((4 * slots + PAD, width), jnp.float32),
            pltpu.VMEM((wide_count, rows, width), jnp.bfloat16),
            pltpu.VMEM((max(COUNTS), width), jnp.float32),
            pltpu.VMEM((4 * rows, fan_in), jnp.bfloat16),
            pltpu.VMEM((block, columns), jnp.bfloat16),
            pltpu.VMEM((fan_in, columns), jnp.bfloat16),
            pltpu.VMEM((columns, fan_in), jnp.bfloat16),
            pltpu.VMEM((4 * rows, columns), jnp.float32),
            pltpu.VMEM((block, columns), jnp.float32),
            pltpu.VMEM((block, columns), jnp.float32),
            pltpu.VMEM((2, 2 * rows, columns), jnp.bfloat16),
            pltpu.VMEM((2, 2 * rows, columns), jnp.bfloat16),
            pltpu.VMEM((2, 4 * rows, columns), jnp.bfloat16),
            pltpu.VMEM((2, 4 * rows, columns), jnp.bfloat16),
            pltpu.VMEM((4, hold, 2 * width), jnp.bfloat16),
            pltpu.VMEM((4, 1, hold), jnp.int32),
            pltpu.VMEM((4, 8, 4 * rows), jnp.float32),
            pltpu.SemaphoreType.DMA((3,)),
            pltpu.SemaphoreType.DMA((2,)),
            pltpu.SemaphoreType.DMA((6,)),
            pltpu.SemaphoreType.DMA((6,)),
            pltpu.SemaphoreType.DMA((chunks,)),
            pltpu.SemaphoreType.DMA((chunks,)),
            *pairs,
            pltpu.SemaphoreType.DMA((4,)),
            pltpu.SemaphoreType.DMA((4,)),
            *[pltpu.SemaphoreType.DMA((3,))] * 4,
        ],
        compiler_params=pltpu.CompilerParams(
            collective_id=1, has_side_effects=True, vmem_limit_bytes=56 << 20
        ),
        cost_estimate=pl.CostEstimate(
            flops=4 * 4 * rows * fan_in * columns,
            bytes_accessed=2 * 2 * fan_in * columns,
            transcendentals=0,
        ),
        name="top_network",
    )(
        lookups,
        lengths,
        cache_table,
        w_first,
        b_first[None],
        w_second,
        b_second[None],
        w_out.astype(jnp.float32)[None],
        miss_rows,
        miss_slots,
        counts,
    )


def copy_kernel(*refs):
    count = len(refs) // 2
    for k in range(count):
        refs[count + k][...] = refs[k][...]


def copied(*arrays):
    vmem = pl.BlockSpec(memory_space=pltpu.VMEM)
    return pl.pallas_call(
        copy_kernel,
        out_shape=tuple(jax.ShapeDtypeStruct(a.shape, a.dtype) for a in arrays),
        in_specs=[vmem] * len(arrays),
        out_specs=(vmem,) * len(arrays),
        name="copied",
    )(*arrays)


def body(
    cache,
    lookup_slots,
    bag_lengths,
    miss_rows,
    miss_slots,
    holder_counts,
    w_first,
    b_first,
    w_second,
    b_second,
    w_out,
):
    top_hidden, logits, cache_next = copied(
        *top_network(
            lookup_slots[0].T,
            bag_lengths,
            cache[0],
            w_first,
            b_first,
            w_second,
            b_second,
            w_out,
            miss_rows[0],
            miss_slots,
            holder_counts[0],
            lax.axis_size("wide"),
        )
    )
    return (top_hidden, logits[0], cache_next[None])


def solution(mesh):
    return jax.shard_map(
        body,
        mesh=mesh,
        in_specs=(
            P("wide", "narrow", None),
            P("wide", None, None),
            P("wide", None),
            P("wide", "narrow", None),
            P("wide", "narrow"),
            P("wide", "narrow"),
            P(None, "narrow"),
            P("narrow"),
            P("narrow", None),
            P("narrow"),
            P("narrow"),
        ),
        out_specs=(P("wide", "narrow"), P("wide"), P("wide", "narrow", None)),
        check_vma=False,
    )
```

```python
import functools

import jax
import jax.numpy as jnp
from jax import lax
from jax.experimental import pallas as pl
from jax.experimental.pallas import tpu as pltpu
from jax.sharding import PartitionSpec as P

COUNTS = (32, 32, 32, 32)
STEPS = 4
PAD = 16
UNROLL = 16
TILE = 256
MESH = pl.DeviceIdType.MESH


def top_kernel(
    lookups_hbm,
    lengths_hbm,
    cache_ref,
    w_first_hbm,
    b_first_ref,
    w_second_hbm,
    b_second_ref,
    w_out_ref,
    miss_rows_ref,
    miss_slots_ref,
    counts_ref,
    top_ref,
    logits_ref,
    cache_next_ref,
    lookups,
    lengths,
    index_ref,
    table,
    wide_table,
    pooled,
    sums,
    features,
    hidden,
    w_first,
    w_second,
    own_part,
    right_part,
    left_part,
    far_out,
    far_in,
    near_out,
    near_in,
    held_rows,
    held_slots,
    logit_parts,
    index_sem,
    weight_sem,
    table_send,
    table_recv,
    exchange_send,
    exchange_recv,
    gather_send,
    gather_recv,
    pass_send,
    pass_recv,
    far_send,
    far_recv,
    near_send,
    near_recv,
    late_send,
    late_recv,
    lone_send,
    lone_recv,
    rows_send,
    rows_recv,
    slots_send,
    slots_recv,
    logit_send,
    logit_recv,
):
    me = lax.axis_index("wide")
    place = lax.axis_index("narrow")
    right, left = lax.rem(place + 1, 4), lax.rem(place + 3, 4)
    slots, width = cache_ref.shape
    wide_count, rows, _ = pooled.shape
    bag_size = lookups.shape[1]
    owner_rows = 4 * rows
    chunks = len(COUNTS)
    starts = tuple(sum(COUNTS[:chunk]) for chunk in range(chunks))
    fan_in, columns = w_first.shape
    sides = ((0, right), (1, left))
    opposite = lax.rem(place + 2, 4)
    everyone = ((0, right), (1, left), (2, opposite))

    def own_span(owner):
        return pl.ds(pl.multiple_of((owner * 4 + place) * rows, rows), rows)

    def fetch(owner, _):
        pltpu.make_async_copy(lookups_hbm.at[:, own_span(owner)], lookups.at[owner], index_sem.at[0]).start()
        return 0

    lax.fori_loop(0, wide_count, fetch, 0)
    lengths_copy = pltpu.make_async_copy(lengths_hbm, lengths, index_sem.at[1])
    lengths_copy.start()
    first_copy = pltpu.make_async_copy(w_first_hbm, w_first, weight_sem.at[0])
    second_copy = pltpu.make_async_copy(w_second_hbm, w_second, weight_sem.at[1])
    first_copy.start()
    second_copy.start()

    barrier = pltpu.get_barrier_semaphore()

    def greet(i, _):
        pl.semaphore_signal(
            barrier, inc=1, device_id={"wide": lax.rem(me + i, wide_count)}, device_id_type=MESH
        )
        return 0

    lax.fori_loop(1, wide_count, greet, 0)
    for _, other in everyone:
        pl.semaphore_signal(barrier, inc=1, device_id={"narrow": other}, device_id_type=MESH)

    hold = miss_rows_ref.shape[0]
    total = counts_ref[0] + counts_ref[1] + counts_ref[2] + counts_ref[3]
    position = lax.broadcasted_iota(jnp.int32, (1, hold), 1)
    held_slots[place] = jnp.where(position < total, miss_slots_ref[...], -1)
    held_rows[:, :, width:] = jnp.ones((4, hold, width), jnp.bfloat16)
    held_rows[place, :, :width] = miss_rows_ref[...]

    pl.semaphore_wait(barrier, wide_count + 2)

    def to_side(source, target, send, recv, other):
        return pltpu.make_async_remote_copy(
            src_ref=source,
            dst_ref=target,
            send_sem=send,
            recv_sem=recv,
            device_id={"narrow": other},
            device_id_type=MESH,
        )

    half = slots // 2
    near_tables = []
    for late in range(2):
        for k, other in sides:
            span = pl.ds((late ^ k) * half, half)
            near_tables.append(
                to_side(
                    cache_ref.at[span],
                    table.at[place, span],
                    table_send.at[2 * late + k],
                    table_recv.at[2 * late + k],
                    other,
                )
            )
    for copy in near_tables:
        copy.start()
    wide_table[pl.ds(pl.multiple_of(place * slots, slots), slots), :] = cache_ref[...].astype(jnp.float32)
    wide_table[4 * slots :, :] = jnp.zeros((PAD, width), jnp.float32)

    pltpu.make_async_copy(lookups, lookups, index_sem.at[0]).wait()
    lengths_copy.wait()

    def mask(owner, _):
        number = lax.broadcasted_iota(jnp.int32, (bag_size, rows), 0)
        lookups[owner] = jnp.where(number < lengths[:, own_span(owner)], lookups[owner], 4 * slots)
        return 0

    lax.fori_loop(0, wide_count, mask, 0)
    index_copy = pltpu.make_async_copy(lookups, index_ref, index_sem.at[2])
    index_copy.start()
    far_tables = []
    for k, other, source in ((0, right, left), (1, left, right)):
        near_tables[k].wait_recv()
        part = table.at[source, pl.ds(k * half, half)]
        copy = to_side(part, part, table_send.at[4 + k], table_recv.at[4 + k], other)
        copy.start()
        far_tables.append(copy)

    def widen(source):
        wide_table[pl.ds(pl.multiple_of(source * slots, slots), slots), :] = table[source].astype(jnp.float32)

    for copy in near_tables[2:]:
        copy.wait_recv()
    widen(left)
    widen(right)
    for copy in far_tables:
        copy.wait_recv()
    widen(opposite)
    index_copy.wait()

    slot_copies = [
        to_side(held_slots.at[place], held_slots.at[place], slots_send.at[k], slots_recv.at[k], other)
        for k, other in everyone
    ]
    own_held = held_rows.at[place, :, pl.ds(0, width)]
    near_held = [
        to_side(own_held, own_held, rows_send.at[k], rows_recv.at[k], other) for k, other in sides
    ]
    for copy in slot_copies + near_held:
        copy.start()
    far_held = []
    for k, other, source in ((0, right, left), (1, left, right)):
        part = held_rows.at[source, pl.ds(k * (hold // 2), hold // 2), pl.ds(0, width)]
        far_held.append(to_side(part, part, rows_send.at[2 + k], rows_recv.at[2 + k], other))

    def pass_held():
        for near, far in zip(near_held, far_held):
            near.wait_recv()
            far.start()

    def held_arrived():
        for copy in slot_copies + far_held:
            copy.wait_recv()

    def refill(low, high):
        def step(t, _):
            span = pl.ds(pl.multiple_of(t * TILE, TILE), TILE)
            slot = place * slots + t * TILE + lax.broadcasted_iota(jnp.int32, (TILE, hold), 0)
            placed = jnp.zeros((TILE, 2 * width), jnp.float32)
            for q in range(4):
                chosen = jnp.where(held_slots[q] == slot, 1.0, 0.0).astype(jnp.bfloat16)
                placed += jnp.dot(chosen, held_rows[q], preferred_element_type=jnp.float32)
            cache_next_ref[span, :] = jnp.where(
                placed[:, width:] > 0.5, placed[:, :width].astype(jnp.bfloat16), cache_ref[span, :]
            )
            return 0

        lax.fori_loop(low, high, step, 0)

    def pool(chunk, low, high):
        count, start = COUNTS[chunk], starts[chunk]

        def owner_step(i, _):
            owner = lax.rem(me + i, wide_count)
            for row in range(0, count, UNROLL):
                for u in range(row, row + UNROLL):
                    terms = [
                        wide_table[pl.ds(index_ref[owner, l, start + u], 1), :] for l in range(bag_size)
                    ]
                    while len(terms) > 1:
                        terms = [terms[k] + terms[k + 1] for k in range(0, len(terms), 2)]
                    sums[pl.ds(u, 1), :] = terms[0]
            source = pooled.at[owner, pl.ds(start, count)]
            source[...] = sums[:count, :].astype(jnp.bfloat16)
            target = features.at[
                pl.ds(pl.multiple_of(4 * start + place * count, 16), count),
                pl.ds(pl.multiple_of(me * width, width), width),
            ]

            @pl.when(i == 0)
            def _():
                pltpu.make_async_copy(source, target, exchange_recv.at[chunk]).start()

            @pl.when(i > 0)
            def _():
                pltpu.make_async_remote_copy(
                    src_ref=source,
                    dst_ref=target,
                    send_sem=exchange_send.at[chunk],
                    recv_sem=exchange_recv.at[chunk],
                    device_id={"wide": owner},
                    device_id_type=MESH,
                ).start()

            return 0

        lax.fori_loop(low, high, owner_step, 0)

    def own_rows(chunk, source):
        return pl.ds(pl.multiple_of(4 * starts[chunk] + source * COUNTS[chunk], 16), COUNTS[chunk])

    def side_halves(chunk, late, send, recv):
        found = []
        for k, other in sides:
            columns_half = pl.ds((late ^ k) * (fan_in // 2), fan_in // 2)
            part = features.at[own_rows(chunk, place), columns_half]
            found.append(to_side(part, part, send.at[chunk, k], recv.at[chunk, k], other))
        return found

    def near_copies(chunk):
        return side_halves(chunk, 0, gather_send, gather_recv)

    def late_copies(chunk):
        return side_halves(chunk, 1, late_send, late_recv)

    def pass_copies(chunk):
        found = []
        for k, other, source in ((0, right, left), (1, left, right)):
            view = features.at[own_rows(chunk, source), pl.ds(k * (fan_in // 2), fan_in // 2)]
            found.append(to_side(view, view, pass_send.at[chunk, k], pass_recv.at[chunk, k], other))
        return found

    def far_copies(chunk):
        span = pl.ds(2 * starts[chunk], 2 * COUNTS[chunk])
        return [
            to_side(far_out.at[k, span], far_in.at[k, span], far_send.at[chunk, k], far_recv.at[chunk, k], other)
            for k, other in sides
        ]

    def sum_halves(chunk, lone, send, recv):
        middle = 2 * COUNTS[chunk]
        found = []
        for k, other in sides:
            span = pl.ds(4 * starts[chunk] + (lone ^ k) * middle, middle)
            found.append(
                to_side(near_out.at[k, span], near_in.at[k, span], send.at[chunk, k], recv.at[chunk, k], other)
            )
        return found

    def near_sums(chunk):
        return sum_halves(chunk, 0, near_send, near_recv)

    def lone_sums(chunk):
        return sum_halves(chunk, 1, lone_send, lone_recv)

    def exchanged(chunk):
        whole = features.at[own_rows(chunk, place)]
        pltpu.make_async_copy(whole, whole, exchange_recv.at[chunk]).wait()
        for copy in near_copies(chunk) + late_copies(chunk):
            copy.start()

    def pass_on(chunk):
        for near, on in zip(near_copies(chunk), pass_copies(chunk)):
            near.wait_recv()
            on.start()

    def layers(chunk):
        block, middle = 4 * COUNTS[chunk], 2 * COUNTS[chunk]
        begin = 4 * starts[chunk]
        for copy in late_copies(chunk) + pass_copies(chunk):
            copy.wait_recv()
        if chunk == 0:
            first_copy.wait()
            second_copy.wait()

        def first(t, _):
            span = pl.ds(pl.multiple_of(t * TILE, TILE), TILE)
            terms = jnp.dot(features[pl.ds(begin, block), :], w_first[:, span], preferred_element_type=jnp.float32)
            hidden[:block, span] = jnp.maximum(terms + b_first_ref[:, span], 0.0).astype(jnp.bfloat16)
            return 0

        lax.fori_loop(0, columns // TILE, first, 0, unroll=True)

        def second(ahead, keep):
            target = lax.rem(place + ahead, 4)

            def step(t, _):
                span = pl.ds(pl.multiple_of(t * TILE, TILE), TILE)
                from_ = pl.ds(pl.multiple_of(target * columns + t * TILE, TILE), TILE)
                keep(span, jnp.dot(hidden[:block, :], w_second[:, from_], preferred_element_type=jnp.float32))
                return 0

            lax.fori_loop(0, columns // TILE, step, 0, unroll=True)

        def keep_far(span, terms):
            for k in range(2):
                half_rows = terms[k * middle : (k + 1) * middle]
                far_out[k, pl.ds(2 * starts[chunk], middle), span] = half_rows.astype(jnp.bfloat16)

        second(2, keep_far)
        for copy in far_copies(chunk):
            copy.start()

        def keep_right(span, terms):
            right_part[:block, span] = terms

        def keep_left(span, terms):
            left_part[:block, span] = terms

        def keep_own(span, terms):
            own_part[pl.ds(begin, block), span] = terms

        second(1, keep_right)
        second(3, keep_left)
        for k, part in enumerate((right_part, left_part)):
            lone = (1 - k) * middle
            near_out[k, pl.ds(begin + lone, middle), :] = part[pl.ds(lone, middle), :].astype(jnp.bfloat16)
        for copy in lone_sums(chunk):
            copy.start()
        second(0, keep_own)

    def join(chunk):
        middle, begin = 2 * COUNTS[chunk], 4 * starts[chunk]
        parts = (right_part, left_part)
        for k, copy in enumerate(far_copies(chunk)):
            copy.wait_recv()
            summed = k * middle
            came = far_in[k, pl.ds(2 * starts[chunk], middle), :].astype(jnp.float32)
            near_out[k, pl.ds(begin + summed, middle), :] = (
                parts[k][pl.ds(summed, middle), :] + came
            ).astype(jnp.bfloat16)
        for copy in near_sums(chunk):
            copy.start()

    def finish(chunk):
        for copy in lone_sums(chunk) + near_sums(chunk):
            copy.wait_recv()
        count = COUNTS[chunk]
        for q in range(4):
            span = pl.ds(4 * starts[chunk] + q * count, count)
            terms = own_part[span, :] + near_in[0, span, :].astype(jnp.float32) + near_in[1, span, :].astype(jnp.float32)
            top_ref[pl.ds(q * rows + starts[chunk], count), :] = jnp.maximum(
                terms + b_second_ref[...], 0.0
            ).astype(jnp.bfloat16)

    part = wide_count // STEPS
    blocks = slots // TILE
    for chunk in range(chunks):
        for step in range(STEPS):
            pool(chunk, step * part, (step + 1) * part)
            if chunk == 0 and step == 1:
                pass_held()
            if step == 0 and chunk >= 1:
                exchanged(chunk - 1)
            if step == 1 and chunk >= 2:
                layers(chunk - 2)
            if step == 2 and chunk >= 1:
                pass_on(chunk - 1)
            if step == 3 and chunk >= 2:
                join(chunk - 2)
            if step == 1 and chunk >= 3:
                finish(chunk - 3)
    last = chunks - 1
    exchanged(last)
    layers(last - 1)
    finish(last - 2)
    pass_on(last)
    join(last - 1)
    held_arrived()
    refill(0, blocks // 2)
    layers(last)
    refill(blocks // 2, blocks)
    join(last)
    finish(last - 1)
    finish(last)

    logit_parts[place] = lax.dot_general(
        jnp.broadcast_to(w_out_ref[...].astype(jnp.float32), (8, columns)).astype(jnp.bfloat16),
        top_ref[...],
        (((1,), (1,)), ((), ())),
        preferred_element_type=jnp.float32,
    )
    logit_copies = [
        to_side(logit_parts.at[place], logit_parts.at[place], logit_send.at[k], logit_recv.at[k], other)
        for k, other in everyone
    ]
    for copy in logit_copies:
        copy.start()
    for chunk in range(chunks):
        sent = pooled.at[pl.ds(0, wide_count - 1), pl.ds(0, COUNTS[chunk])]
        pltpu.make_async_copy(sent, sent, exchange_send.at[chunk]).wait()
        for copies in (near_copies, late_copies, pass_copies, far_copies, lone_sums, near_sums):
            for copy in copies(chunk):
                copy.wait_send()
    for copy in near_tables + far_tables + slot_copies + near_held + far_held:
        copy.wait_send()
    for copy in logit_copies:
        copy.wait_recv()
    logits_ref[...] = (
        logit_parts[0][:1] + logit_parts[1][:1] + (logit_parts[2][:1] + logit_parts[3][:1])
    )
    for copy in logit_copies:
        copy.wait_send()


def top_network(
    lookups,
    lengths,
    cache_table,
    w_first,
    b_first,
    w_second,
    b_second,
    w_out,
    miss_rows,
    miss_slots,
    counts,
    wide_count,
):
    slots, width = cache_table.shape
    bag_size, batch_rows = lookups.shape
    rows = batch_rows // (4 * wide_count)
    chunks = len(COUNTS)
    block = 4 * max(COUNTS)
    fan_in, columns = w_first.shape
    vmem = pl.BlockSpec(memory_space=pltpu.VMEM)
    hbm = pl.BlockSpec(memory_space=pl.ANY)
    smem = pl.BlockSpec(memory_space=pltpu.SMEM)
    hold = miss_rows.shape[0]
    pairs = [pltpu.SemaphoreType.DMA((chunks, 2))] * 12
    return pl.pallas_call(
        top_kernel,
        out_shape=(
            jax.ShapeDtypeStruct((4 * rows, columns), jnp.bfloat16),
            jax.ShapeDtypeStruct((1, 4 * rows), jnp.float32),
            jax.ShapeDtypeStruct((slots, width), jnp.bfloat16),
        ),
        in_specs=[hbm, hbm, vmem, hbm, vmem, hbm, vmem, vmem, vmem, vmem, smem],
        out_specs=(vmem, vmem, vmem),
        scratch_shapes=[
            pltpu.VMEM((wide_count, bag_size, rows), jnp.int32),
            pltpu.VMEM((1, batch_rows), jnp.int32),
            pltpu.SMEM((wide_count, bag_size, rows), jnp.int32),
            pltpu.VMEM((4, slots, width), jnp.bfloat16),
            pltpu.VMEM((4 * slots + PAD, width), jnp.float32),
            pltpu.VMEM((wide_count, rows, width), jnp.bfloat16),
            pltpu.VMEM((max(COUNTS), width), jnp.float32),
            pltpu.VMEM((4 * rows, fan_in), jnp.bfloat16),
            pltpu.VMEM((block, columns), jnp.bfloat16),
            pltpu.VMEM((fan_in, columns), jnp.bfloat16),
            pltpu.VMEM((columns, fan_in), jnp.bfloat16),
            pltpu.VMEM((4 * rows, columns), jnp.float32),
            pltpu.VMEM((block, columns), jnp.float32),
            pltpu.VMEM((block, columns), jnp.float32),
            pltpu.VMEM((2, 2 * rows, columns), jnp.bfloat16),
            pltpu.VMEM((2, 2 * rows, columns), jnp.bfloat16),
            pltpu.VMEM((2, 4 * rows, columns), jnp.bfloat16),
            pltpu.VMEM((2, 4 * rows, columns), jnp.bfloat16),
            pltpu.VMEM((4, hold, 2 * width), jnp.bfloat16),
            pltpu.VMEM((4, 1, hold), jnp.int32),
            pltpu.VMEM((4, 8, 4 * rows), jnp.float32),
            pltpu.SemaphoreType.DMA((3,)),
            pltpu.SemaphoreType.DMA((2,)),
            pltpu.SemaphoreType.DMA((6,)),
            pltpu.SemaphoreType.DMA((6,)),
            pltpu.SemaphoreType.DMA((chunks,)),
            pltpu.SemaphoreType.DMA((chunks,)),
            *pairs,
            pltpu.SemaphoreType.DMA((4,)),
            pltpu.SemaphoreType.DMA((4,)),
            *[pltpu.SemaphoreType.DMA((3,))] * 4,
        ],
        compiler_params=pltpu.CompilerParams(
            collective_id=1, has_side_effects=True, vmem_limit_bytes=56 << 20
        ),
        cost_estimate=pl.CostEstimate(
            flops=4 * 4 * rows * fan_in * columns,
            bytes_accessed=2 * 2 * fan_in * columns,
            transcendentals=0,
        ),
        name="top_network",
    )(
        lookups,
        lengths,
        cache_table,
        w_first,
        b_first[None],
        w_second,
        b_second[None],
        w_out[None],
        miss_rows,
        miss_slots,
        counts,
    )


def copy_kernel(count, *refs):
    sources, targets, held = refs[:count], refs[count : 2 * count], refs[2 * count : 3 * count]
    sems = refs[3 * count]
    ins = [pltpu.make_async_copy(sources[k], held[k], sems.at[0, k]) for k in range(count)]
    outs = [pltpu.make_async_copy(held[k], targets[k], sems.at[1, k]) for k in range(count)]
    for copy in ins:
        copy.start()
    for arrived, leave in zip(ins, outs):
        arrived.wait()
        leave.start()
    for copy in outs:
        copy.wait()


def copied(*arrays):
    hbm = pl.BlockSpec(memory_space=pl.ANY)
    count = len(arrays)
    return pl.pallas_call(
        functools.partial(copy_kernel, count),
        out_shape=tuple(jax.ShapeDtypeStruct(a.shape, a.dtype) for a in arrays),
        in_specs=[hbm] * count,
        out_specs=(hbm,) * count,
        scratch_shapes=[
            *[pltpu.VMEM(a.shape, a.dtype) for a in arrays],
            pltpu.SemaphoreType.DMA((2, count)),
        ],
        name="copied",
    )(*arrays)


def body(
    cache,
    lookup_slots,
    bag_lengths,
    miss_rows,
    miss_slots,
    holder_counts,
    w_first,
    b_first,
    w_second,
    b_second,
    w_out,
):
    top_hidden, logits, cache_next = copied(
        *top_network(
            lookup_slots[0].T,
            bag_lengths,
            cache[0],
            w_first,
            b_first,
            w_second,
            b_second,
            w_out,
            miss_rows[0],
            miss_slots,
            holder_counts[0],
            lax.axis_size("wide"),
        )
    )
    return (top_hidden, logits[0], cache_next[None])


def solution(mesh):
    return jax.shard_map(
        body,
        mesh=mesh,
        in_specs=(
            P("wide", "narrow", None),
            P("wide", None, None),
            P("wide", None),
            P("wide", "narrow", None),
            P("wide", "narrow"),
            P("wide", "narrow"),
            P(None, "narrow"),
            P("narrow"),
            P("narrow", None),
            P("narrow"),
            P("narrow"),
        ),
        out_specs=(P("wide", "narrow"), P("wide"), P("wide", "narrow", None)),
        check_vma=False,
    )
```

```python
import functools

import jax
import jax.numpy as jnp
from jax import lax
from jax.experimental import pallas as pl
from jax.experimental.pallas import tpu as pltpu
from jax.sharding import PartitionSpec as P

COUNTS = (32, 32, 32, 32)
STEPS = 4
PAD = 16
UNROLL = 16
TILE = 256
MESH = pl.DeviceIdType.MESH


def top_kernel(
    lookups_hbm,
    lengths_hbm,
    cache_ref,
    w_first_hbm,
    b_first_ref,
    w_second_hbm,
    b_second_ref,
    w_out_ref,
    miss_rows_ref,
    miss_slots_ref,
    counts_ref,
    top_ref,
    logits_ref,
    cache_next_ref,
    lookups,
    lengths,
    index_ref,
    table,
    wide_table,
    pooled,
    sums,
    features,
    hidden,
    w_first,
    w_second,
    own_part,
    right_part,
    left_part,
    far_out,
    far_in,
    near_out,
    near_in,
    held_rows,
    held_slots,
    logit_parts,
    index_sem,
    weight_sem,
    table_send,
    table_recv,
    exchange_send,
    exchange_recv,
    gather_send,
    gather_recv,
    pass_send,
    pass_recv,
    far_send,
    far_recv,
    near_send,
    near_recv,
    late_send,
    late_recv,
    lone_send,
    lone_recv,
    rows_send,
    rows_recv,
    slots_send,
    slots_recv,
    logit_send,
    logit_recv,
):
    me = lax.axis_index("wide")
    place = lax.axis_index("narrow")
    right, left = lax.rem(place + 1, 4), lax.rem(place + 3, 4)
    slots, width = cache_ref.shape
    wide_count, rows, _ = pooled.shape
    bag_size = lookups.shape[1]
    owner_rows = 4 * rows
    chunks = len(COUNTS)
    starts = tuple(sum(COUNTS[:chunk]) for chunk in range(chunks))
    fan_in, columns = w_first.shape
    sides = ((0, right), (1, left))
    opposite = lax.rem(place + 2, 4)
    everyone = ((0, right), (1, left), (2, opposite))

    def own_span(owner):
        return pl.ds(pl.multiple_of((owner * 4 + place) * rows, rows), rows)

    def fetch(owner, _):
        pltpu.make_async_copy(lookups_hbm.at[:, own_span(owner)], lookups.at[owner], index_sem.at[0]).start()
        return 0

    lax.fori_loop(0, wide_count, fetch, 0)
    lengths_copy = pltpu.make_async_copy(lengths_hbm, lengths, index_sem.at[1])
    lengths_copy.start()
    first_copy = pltpu.make_async_copy(w_first_hbm, w_first, weight_sem.at[0])
    second_copy = pltpu.make_async_copy(w_second_hbm, w_second, weight_sem.at[1])
    first_copy.start()
    second_copy.start()

    barrier = pltpu.get_barrier_semaphore()

    def greet(i, _):
        pl.semaphore_signal(
            barrier, inc=1, device_id={"wide": lax.rem(me + i, wide_count)}, device_id_type=MESH
        )
        return 0

    lax.fori_loop(1, wide_count, greet, 0)
    for _, other in everyone:
        pl.semaphore_signal(barrier, inc=1, device_id={"narrow": other}, device_id_type=MESH)

    hold = miss_rows_ref.shape[0]
    total = counts_ref[0] + counts_ref[1] + counts_ref[2] + counts_ref[3]
    position = lax.broadcasted_iota(jnp.int32, (1, hold), 1)
    held_slots[place] = jnp.where(position < total, miss_slots_ref[...], -1)
    held_rows[:, :, width:] = jnp.ones((4, hold, width), jnp.bfloat16)
    held_rows[place, :, :width] = miss_rows_ref[...]

    pl.semaphore_wait(barrier, wide_count + 2)

    def to_side(source, target, send, recv, other):
        return pltpu.make_async_remote_copy(
            src_ref=source,
            dst_ref=target,
            send_sem=send,
            recv_sem=recv,
            device_id={"narrow": other},
            device_id_type=MESH,
        )

    half = slots // 2
    near_tables = []
    for late in range(2):
        for k, other in sides:
            span = pl.ds((late ^ k) * half, half)
            near_tables.append(
                to_side(
                    cache_ref.at[span],
                    table.at[place, span],
                    table_send.at[2 * late + k],
                    table_recv.at[2 * late + k],
                    other,
                )
            )
    for copy in near_tables:
        copy.start()
    wide_table[pl.ds(pl.multiple_of(place * slots, slots), slots), :] = cache_ref[...].astype(jnp.float32)
    wide_table[4 * slots :, :] = jnp.zeros((PAD, width), jnp.float32)

    pltpu.make_async_copy(lookups, lookups, index_sem.at[0]).wait()
    lengths_copy.wait()

    def mask(owner, _):
        number = lax.broadcasted_iota(jnp.int32, (bag_size, rows), 0)
        lookups[owner] = jnp.where(number < lengths[:, own_span(owner)], lookups[owner], 4 * slots)
        return 0

    lax.fori_loop(0, wide_count, mask, 0)
    index_copy = pltpu.make_async_copy(lookups, index_ref, index_sem.at[2])
    index_copy.start()
    far_tables = []
    for k, other, source in ((0, right, left), (1, left, right)):
        near_tables[k].wait_recv()
        part = table.at[source, pl.ds(k * half, half)]
        copy = to_side(part, part, table_send.at[4 + k], table_recv.at[4 + k], other)
        copy.start()
        far_tables.append(copy)

    def widen(source):
        wide_table[pl.ds(pl.multiple_of(source * slots, slots), slots), :] = table[source].astype(jnp.float32)

    for copy in near_tables[2:]:
        copy.wait_recv()
    widen(left)
    widen(right)
    for copy in far_tables:
        copy.wait_recv()
    widen(opposite)
    index_copy.wait()

    slot_copies = [
        to_side(held_slots.at[place], held_slots.at[place], slots_send.at[k], slots_recv.at[k], other)
        for k, other in everyone
    ]
    own_held = held_rows.at[place, :, pl.ds(0, width)]
    near_held = [
        to_side(own_held, own_held, rows_send.at[k], rows_recv.at[k], other) for k, other in sides
    ]
    for copy in slot_copies + near_held:
        copy.start()
    far_held = []
    for k, other, source in ((0, right, left), (1, left, right)):
        part = held_rows.at[source, pl.ds(k * (hold // 2), hold // 2), pl.ds(0, width)]
        far_held.append(to_side(part, part, rows_send.at[2 + k], rows_recv.at[2 + k], other))

    def pass_held():
        for near, far in zip(near_held, far_held):
            near.wait_recv()
            far.start()

    def held_arrived():
        for copy in slot_copies + far_held:
            copy.wait_recv()

    def refill(low, high):
        def step(t, _):
            span = pl.ds(pl.multiple_of(t * TILE, TILE), TILE)
            slot = place * slots + t * TILE + lax.broadcasted_iota(jnp.int32, (TILE, hold), 0)
            placed = jnp.zeros((TILE, 2 * width), jnp.float32)
            for q in range(4):
                chosen = jnp.where(held_slots[q] == slot, 1.0, 0.0).astype(jnp.bfloat16)
                placed += jnp.dot(chosen, held_rows[q], preferred_element_type=jnp.float32)
            cache_next_ref[span, :] = jnp.where(
                placed[:, width:] > 0.5, placed[:, :width].astype(jnp.bfloat16), cache_ref[span, :]
            )
            return 0

        lax.fori_loop(low, high, step, 0)

    def pool(chunk, low, high):
        count, start = COUNTS[chunk], starts[chunk]

        def owner_step(i, _):
            owner = lax.rem(me + i, wide_count)
            for row in range(0, count, UNROLL):
                for u in range(row, row + UNROLL):
                    terms = [
                        wide_table[pl.ds(index_ref[owner, l, start + u], 1), :] for l in range(bag_size)
                    ]
                    while len(terms) > 1:
                        terms = [terms[k] + terms[k + 1] for k in range(0, len(terms), 2)]
                    sums[pl.ds(u, 1), :] = terms[0]
            source = pooled.at[owner, pl.ds(start, count)]
            source[...] = sums[:count, :].astype(jnp.bfloat16)
            target = features.at[
                pl.ds(pl.multiple_of(4 * start + place * count, 16), count),
                pl.ds(pl.multiple_of(me * width, width), width),
            ]

            @pl.when(i == 0)
            def _():
                pltpu.make_async_copy(source, target, exchange_recv.at[chunk]).start()

            @pl.when(i > 0)
            def _():
                pltpu.make_async_remote_copy(
                    src_ref=source,
                    dst_ref=target,
                    send_sem=exchange_send.at[chunk],
                    recv_sem=exchange_recv.at[chunk],
                    device_id={"wide": owner},
                    device_id_type=MESH,
                ).start()

            return 0

        lax.fori_loop(low, high, owner_step, 0)

    def own_rows(chunk, source):
        return pl.ds(pl.multiple_of(4 * starts[chunk] + source * COUNTS[chunk], 16), COUNTS[chunk])

    def side_halves(chunk, late, send, recv):
        found = []
        for k, other in sides:
            columns_half = pl.ds((late ^ k) * (fan_in // 2), fan_in // 2)
            part = features.at[own_rows(chunk, place), columns_half]
            found.append(to_side(part, part, send.at[chunk, k], recv.at[chunk, k], other))
        return found

    def near_copies(chunk):
        return side_halves(chunk, 0, gather_send, gather_recv)

    def late_copies(chunk):
        return side_halves(chunk, 1, late_send, late_recv)

    def pass_copies(chunk):
        found = []
        for k, other, source in ((0, right, left), (1, left, right)):
            view = features.at[own_rows(chunk, source), pl.ds(k * (fan_in // 2), fan_in // 2)]
            found.append(to_side(view, view, pass_send.at[chunk, k], pass_recv.at[chunk, k], other))
        return found

    def far_copies(chunk):
        span = pl.ds(2 * starts[chunk], 2 * COUNTS[chunk])
        return [
            to_side(far_out.at[k, span], far_in.at[k, span], far_send.at[chunk, k], far_recv.at[chunk, k], other)
            for k, other in sides
        ]

    def sum_halves(chunk, lone, send, recv):
        middle = 2 * COUNTS[chunk]
        found = []
        for k, other in sides:
            span = pl.ds(4 * starts[chunk] + (lone ^ k) * middle, middle)
            found.append(
                to_side(near_out.at[k, span], near_in.at[k, span], send.at[chunk, k], recv.at[chunk, k], other)
            )
        return found

    def near_sums(chunk):
        return sum_halves(chunk, 0, near_send, near_recv)

    def lone_sums(chunk):
        return sum_halves(chunk, 1, lone_send, lone_recv)

    def exchanged(chunk):
        whole = features.at[own_rows(chunk, place)]
        pltpu.make_async_copy(whole, whole, exchange_recv.at[chunk]).wait()
        for copy in near_copies(chunk) + late_copies(chunk):
            copy.start()

    def pass_on(chunk):
        for near, on in zip(near_copies(chunk), pass_copies(chunk)):
            near.wait_recv()
            on.start()

    def layers(chunk):
        block, middle = 4 * COUNTS[chunk], 2 * COUNTS[chunk]
        begin = 4 * starts[chunk]
        for copy in late_copies(chunk) + pass_copies(chunk):
            copy.wait_recv()
        if chunk == 0:
            first_copy.wait()
            second_copy.wait()

        def first(t, _):
            span = pl.ds(pl.multiple_of(t * TILE, TILE), TILE)
            terms = jnp.dot(features[pl.ds(begin, block), :], w_first[:, span], preferred_element_type=jnp.float32)
            hidden[:block, span] = jnp.maximum(terms + b_first_ref[:, span], 0.0).astype(jnp.bfloat16)
            return 0

        lax.fori_loop(0, columns // TILE, first, 0, unroll=True)

        def second(ahead, keep):
            target = lax.rem(place + ahead, 4)

            def step(t, _):
                span = pl.ds(pl.multiple_of(t * TILE, TILE), TILE)
                from_ = pl.ds(pl.multiple_of(target * columns + t * TILE, TILE), TILE)
                keep(span, jnp.dot(hidden[:block, :], w_second[:, from_], preferred_element_type=jnp.float32))
                return 0

            lax.fori_loop(0, columns // TILE, step, 0, unroll=True)

        def keep_far(span, terms):
            for k in range(2):
                half_rows = terms[k * middle : (k + 1) * middle]
                far_out[k, pl.ds(2 * starts[chunk], middle), span] = half_rows.astype(jnp.bfloat16)

        second(2, keep_far)
        for copy in far_copies(chunk):
            copy.start()

        def keep_right(span, terms):
            right_part[:block, span] = terms

        def keep_left(span, terms):
            left_part[:block, span] = terms

        def keep_own(span, terms):
            own_part[pl.ds(begin, block), span] = terms

        second(1, keep_right)
        second(3, keep_left)
        for k, part in enumerate((right_part, left_part)):
            lone = (1 - k) * middle
            near_out[k, pl.ds(begin + lone, middle), :] = part[pl.ds(lone, middle), :].astype(jnp.bfloat16)
        for copy in lone_sums(chunk):
            copy.start()
        second(0, keep_own)

    def join(chunk):
        middle, begin = 2 * COUNTS[chunk], 4 * starts[chunk]
        parts = (right_part, left_part)
        onward = near_sums(chunk)
        for k, copy in enumerate(far_copies(chunk)):
            copy.wait_recv()
            summed = k * middle
            came = far_in[k, pl.ds(2 * starts[chunk], middle), :].astype(jnp.float32)
            near_out[k, pl.ds(begin + summed, middle), :] = (
                parts[k][pl.ds(summed, middle), :] + came
            ).astype(jnp.bfloat16)
            onward[k].start()

    def finish(chunk):
        for copy in lone_sums(chunk) + near_sums(chunk):
            copy.wait_recv()
        count = COUNTS[chunk]
        for q in range(4):
            span = pl.ds(4 * starts[chunk] + q * count, count)
            terms = own_part[span, :] + near_in[0, span, :].astype(jnp.float32) + near_in[1, span, :].astype(jnp.float32)
            top_ref[pl.ds(q * rows + starts[chunk], count), :] = jnp.maximum(
                terms + b_second_ref[...], 0.0
            ).astype(jnp.bfloat16)

    part = wide_count // STEPS
    blocks = slots // TILE
    for chunk in range(chunks):
        for step in range(STEPS):
            pool(chunk, step * part, (step + 1) * part)
            if chunk == 0 and step == 1:
                pass_held()
            if step == 0 and chunk >= 1:
                exchanged(chunk - 1)
            if step == 1 and chunk >= 2:
                layers(chunk - 2)
            if step == 2 and chunk >= 1:
                pass_on(chunk - 1)
            if step == 3 and chunk >= 2:
                join(chunk - 2)
            if step == 1 and chunk >= 3:
                finish(chunk - 3)
    last = chunks - 1
    exchanged(last)
    layers(last - 1)
    finish(last - 2)
    pass_on(last)
    join(last - 1)
    held_arrived()
    refill(0, blocks // 2)
    layers(last)
    refill(blocks // 2, blocks)
    join(last)
    finish(last - 1)
    finish(last)

    logit_parts[place] = lax.dot_general(
        jnp.broadcast_to(w_out_ref[...].astype(jnp.float32), (8, columns)).astype(jnp.bfloat16),
        top_ref[...],
        (((1,), (1,)), ((), ())),
        preferred_element_type=jnp.float32,
    )
    logit_copies = [
        to_side(logit_parts.at[place], logit_parts.at[place], logit_send.at[k], logit_recv.at[k], other)
        for k, other in everyone
    ]
    for copy in logit_copies:
        copy.start()
    for chunk in range(chunks):
        sent = pooled.at[pl.ds(0, wide_count - 1), pl.ds(0, COUNTS[chunk])]
        pltpu.make_async_copy(sent, sent, exchange_send.at[chunk]).wait()
        for copies in (near_copies, late_copies, pass_copies, far_copies, lone_sums, near_sums):
            for copy in copies(chunk):
                copy.wait_send()
    for copy in near_tables + far_tables + slot_copies + near_held + far_held:
        copy.wait_send()
    for copy in logit_copies:
        copy.wait_recv()
    logits_ref[...] = (
        logit_parts[0][:1] + logit_parts[1][:1] + (logit_parts[2][:1] + logit_parts[3][:1])
    )
    for copy in logit_copies:
        copy.wait_send()


def top_network(
    lookups,
    lengths,
    cache_table,
    w_first,
    b_first,
    w_second,
    b_second,
    w_out,
    miss_rows,
    miss_slots,
    counts,
    wide_count,
):
    slots, width = cache_table.shape
    bag_size, batch_rows = lookups.shape
    rows = batch_rows // (4 * wide_count)
    chunks = len(COUNTS)
    block = 4 * max(COUNTS)
    fan_in, columns = w_first.shape
    vmem = pl.BlockSpec(memory_space=pltpu.VMEM)
    hbm = pl.BlockSpec(memory_space=pl.ANY)
    smem = pl.BlockSpec(memory_space=pltpu.SMEM)
    hold = miss_rows.shape[0]
    pairs = [pltpu.SemaphoreType.DMA((chunks, 2))] * 12
    return pl.pallas_call(
        top_kernel,
        out_shape=(
            jax.ShapeDtypeStruct((4 * rows, columns), jnp.bfloat16),
            jax.ShapeDtypeStruct((1, 4 * rows), jnp.float32),
            jax.ShapeDtypeStruct((slots, width), jnp.bfloat16),
        ),
        in_specs=[hbm, hbm, vmem, hbm, vmem, hbm, vmem, vmem, vmem, vmem, smem],
        out_specs=(vmem, vmem, vmem),
        scratch_shapes=[
            pltpu.VMEM((wide_count, bag_size, rows), jnp.int32),
            pltpu.VMEM((1, batch_rows), jnp.int32),
            pltpu.SMEM((wide_count, bag_size, rows), jnp.int32),
            pltpu.VMEM((4, slots, width), jnp.bfloat16),
            pltpu.VMEM((4 * slots + PAD, width), jnp.float32),
            pltpu.VMEM((wide_count, rows, width), jnp.bfloat16),
            pltpu.VMEM((max(COUNTS), width), jnp.float32),
            pltpu.VMEM((4 * rows, fan_in), jnp.bfloat16),
            pltpu.VMEM((block, columns), jnp.bfloat16),
            pltpu.VMEM((fan_in, columns), jnp.bfloat16),
            pltpu.VMEM((columns, fan_in), jnp.bfloat16),
            pltpu.VMEM((4 * rows, columns), jnp.float32),
            pltpu.VMEM((block, columns), jnp.float32),
            pltpu.VMEM((block, columns), jnp.float32),
            pltpu.VMEM((2, 2 * rows, columns), jnp.bfloat16),
            pltpu.VMEM((2, 2 * rows, columns), jnp.bfloat16),
            pltpu.VMEM((2, 4 * rows, columns), jnp.bfloat16),
            pltpu.VMEM((2, 4 * rows, columns), jnp.bfloat16),
            pltpu.VMEM((4, hold, 2 * width), jnp.bfloat16),
            pltpu.VMEM((4, 1, hold), jnp.int32),
            pltpu.VMEM((4, 8, 4 * rows), jnp.float32),
            pltpu.SemaphoreType.DMA((3,)),
            pltpu.SemaphoreType.DMA((2,)),
            pltpu.SemaphoreType.DMA((6,)),
            pltpu.SemaphoreType.DMA((6,)),
            pltpu.SemaphoreType.DMA((chunks,)),
            pltpu.SemaphoreType.DMA((chunks,)),
            *pairs,
            pltpu.SemaphoreType.DMA((4,)),
            pltpu.SemaphoreType.DMA((4,)),
            *[pltpu.SemaphoreType.DMA((3,))] * 4,
        ],
        compiler_params=pltpu.CompilerParams(
            collective_id=1, has_side_effects=True, vmem_limit_bytes=56 << 20
        ),
        cost_estimate=pl.CostEstimate(
            flops=4 * 4 * rows * fan_in * columns,
            bytes_accessed=2 * 2 * fan_in * columns,
            transcendentals=0,
        ),
        name="top_network",
    )(
        lookups,
        lengths,
        cache_table,
        w_first,
        b_first[None],
        w_second,
        b_second[None],
        w_out[None],
        miss_rows,
        miss_slots,
        counts,
    )


def copy_kernel(count, *refs):
    sources, targets, held = refs[:count], refs[count : 2 * count], refs[2 * count : 3 * count]
    sems = refs[3 * count]
    ins = [pltpu.make_async_copy(sources[k], held[k], sems.at[0, k]) for k in range(count)]
    outs = [pltpu.make_async_copy(held[k], targets[k], sems.at[1, k]) for k in range(count)]
    for copy in ins:
        copy.start()
    for arrived, leave in zip(ins, outs):
        arrived.wait()
        leave.start()
    for copy in outs:
        copy.wait()


def copied(*arrays):
    hbm = pl.BlockSpec(memory_space=pl.ANY)
    count = len(arrays)
    return pl.pallas_call(
        functools.partial(copy_kernel, count),
        out_shape=tuple(jax.ShapeDtypeStruct(a.shape, a.dtype) for a in arrays),
        in_specs=[hbm] * count,
        out_specs=(hbm,) * count,
        scratch_shapes=[
            *[pltpu.VMEM(a.shape, a.dtype) for a in arrays],
            pltpu.SemaphoreType.DMA((2, count)),
        ],
        name="copied",
    )(*arrays)


def body(
    cache,
    lookup_slots,
    bag_lengths,
    miss_rows,
    miss_slots,
    holder_counts,
    w_first,
    b_first,
    w_second,
    b_second,
    w_out,
):
    top_hidden, logits, cache_next = copied(
        *top_network(
            lookup_slots[0].T,
            bag_lengths,
            cache[0],
            w_first,
            b_first,
            w_second,
            b_second,
            w_out,
            miss_rows[0],
            miss_slots,
            holder_counts[0],
            lax.axis_size("wide"),
        )
    )
    return (top_hidden, logits[0], cache_next[None])


def solution(mesh):
    return jax.shard_map(
        body,
        mesh=mesh,
        in_specs=(
            P("wide", "narrow", None),
            P("wide", None, None),
            P("wide", None),
            P("wide", "narrow", None),
            P("wide", "narrow"),
            P("wide", "narrow"),
            P(None, "narrow"),
            P("narrow"),
            P("narrow", None),
            P("narrow"),
            P("narrow"),
        ),
        out_specs=(P("wide", "narrow"), P("wide"), P("wide", "narrow", None)),
        check_vma=False,
    )
```
